128 devices in a mesh: grp: 4 (over y), dev: 32 (over x, z, core).
Axes of the slice: x: 4, y: 4, z: 4, core: 2. Of those that a mesh axis runs over, the one named last changes fastest.
Arguments:
- tokens: bfloat16 [4096, 3584], P(('grp', 'dev')), may hold values from -6 to 6
- expert_ids: int32 [4096, 8], P(('grp', 'dev')), may hold values from 0 to 127, all different within a row; in each aligned block of 32 rows (0 to 31, 32 to 63, ...) at most 4 rows name the same one
- gate_weights: float32 [4096, 8], P(('grp', 'dev')), may hold values from 0.1 to 0.6
- expert_gate: bfloat16 [128, 3584, 1024], P(('grp', 'dev')), may hold values from -0.09375 to 0.09375
- expert_up: bfloat16 [128, 3584, 1024], P(('grp', 'dev')), may hold values from -0.09375 to 0.09375
- expert_down: bfloat16 [128, 1024, 3584], P(('grp', 'dev')), may hold values from -0.1875 to 0.1875
- pool_latent: bfloat16 [2048, 64, 512], P(('grp', 'dev')), may hold values from -4 to 4
- pool_rope: bfloat16 [2048, 4096], P(('grp', 'dev')), may hold values from -4 to 4
- page_owner: int32 [2048, 16], P(('grp', 'dev')), may hold values from 0 to 127, as said below
- page_index: int32 [2048, 16], P(('grp', 'dev')), may hold values from 0 to 15, as said below
- lengths: int32 [2048], P(('grp', 'dev')), may hold values from 1 to 1024, as said below
- query_latent: bfloat16 [2048, 64, 512], P(('grp', 'dev')), may hold values from -128 to 128
- query_rope: bfloat16 [2048, 4096], P(('grp', 'dev')), may hold values from -128 to 128
- new_latent: bfloat16 [2048, 512], P(('grp', 'dev')), may hold values from -4 to 4
- new_rope: bfloat16 [2048, 64], P(('grp', 'dev')), may hold values from -4 to 4
Outputs:
- moe_out: bfloat16 [4096, 3584], P(('grp', 'dev'))
- attn_latent: bfloat16 [2048, 64, 512], P(('grp', 'dev'))
The draws below stay inside these ranges and needn't reach their ends.
Inputs may be any that keep to these rules, and one draw needn't show every extreme that they name: `page_owner`: among one device's 16 x 16 entries every device of grp+dev, counted by its index along grp+dev, is named exactly 2 times, and exactly 1 times among the entries in use (slot p of session s with p * 64 < lengths[s]). `page_index`: a page of the owner's pool. `lengths`: positions cached before the new token; page slots at or beyond the length in pages are listed but not read; the pages in use of one device's sessions number exactly 128; on every device some session has exactly 1024. `expert_ids`: in the rows of one device an expert is named at most 4 times.
All inputs are finite; a program needn't handle non-finite values.
Results may differ from the reference program's by a relative error of at most 0.0058.
Values may be sent and summed in bfloat16 or wider, within the bound.
A program may use at most 192 MiB of HBM per device.

```python
import math
import jax
import jax.numpy as jnp
import numpy as np
from jax import lax

D = 3584
FF = 1024
HEADS = 64
KV = 512
ROPE = 64
PAGE = 64
TOP = 8
PMAX = 16
POOL = 16
ROWS = 32
SESS = 16
EXPERTS = 128
TOKENS = 4096
SESSIONS = 2048
POOLS = 2048
CAP = 4
LMAX = 1024


def pool_page(base_key, page_row):
    return jax.random.truncated_normal(jax.random.fold_in(base_key, page_row), -4.0, 4.0, (PAGE, KV), jnp.float32)


def rope_page(base_key, page_row):
    return jax.random.truncated_normal(jax.random.fold_in(base_key, page_row), -4.0, 4.0, (PAGE * ROPE,), jnp.float32)


def latent_pool(key):
    base_key = jax.random.fold_in(key, 101)

    def one_page(page_row):
        return pool_page(base_key, page_row)
    return jax.vmap(one_page)(jnp.arange(POOLS, dtype=jnp.int32))


def rope_pool(key):
    base_key = jax.random.fold_in(key, 102)

    def one_page(page_row):
        return rope_page(base_key, page_row)
    return jax.vmap(one_page)(jnp.arange(POOLS, dtype=jnp.int32))


def new_latents(key):
    return jax.random.truncated_normal(jax.random.fold_in(key, 103), -4.0, 4.0, (SESSIONS, KV), jnp.float32)


def new_ropes(key):
    return jax.random.truncated_normal(jax.random.fold_in(key, 104), -4.0, 4.0, (SESSIONS, ROPE), jnp.float32)


def page_counts(key):
    base_key = jax.random.fold_in(key, 120)
    devices = SESSIONS // SESS
    pattern = jnp.tile(jnp.array([1, 3, 5, 7, 9, 11, 12, 16], jnp.int32), SESS // 8)

    def one_device(device_index):
        return jax.random.permutation(jax.random.fold_in(base_key, device_index), pattern)
    return jax.vmap(one_device)(jnp.arange(devices, dtype=jnp.int32))


def owner_table(key):
    base_key = jax.random.fold_in(key, 105)
    devices = SESSIONS // SESS
    counts = page_counts(key)
    in_use = (jnp.arange(PMAX, dtype=jnp.int32)[None, None, :] < counts[:, :, None]).astype(jnp.int32).reshape(devices, SESS * PMAX)
    unused = 1 - in_use
    use_rank = jnp.cumsum(in_use, axis=1) - in_use
    free_rank = jnp.cumsum(unused, axis=1) - unused
    owner_cycle = jnp.arange(SESS * PMAX // 2, dtype=jnp.int32) % devices

    def one_device(device_index):
        first = jax.random.permutation(jax.random.fold_in(base_key, 2 * device_index), owner_cycle)
        second = jax.random.permutation(jax.random.fold_in(base_key, 2 * device_index + 1), owner_cycle)
        return (first, second)
    first_cycle, second_cycle = jax.vmap(one_device)(jnp.arange(devices, dtype=jnp.int32))
    from_first = jnp.take_along_axis(first_cycle, jnp.minimum(use_rank, SESS * PMAX // 2 - 1), axis=1)
    from_second = jnp.take_along_axis(second_cycle, jnp.minimum(free_rank, SESS * PMAX // 2 - 1), axis=1)
    owners = jnp.where(in_use == 1, from_first, from_second)
    return owners.reshape(SESSIONS, PMAX).astype(jnp.int32)


def index_table(key):
    return jax.random.randint(jax.random.fold_in(key, 106), (SESSIONS, PMAX), 0, POOL, dtype=jnp.int32)


def draw_pool_latent(key, part):
    return latent_pool(key).astype(jnp.bfloat16)


def draw_pool_rope(key, part):
    return rope_pool(key).astype(jnp.bfloat16)


def draw_page_owner(key, part):
    return owner_table(key)


def draw_page_index(key, part):
    return index_table(key)


def draw_new_latent(key, part):
    return new_latents(key).astype(jnp.bfloat16)


def draw_new_rope(key, part):
    return new_ropes(key).astype(jnp.bfloat16)


def draw_lengths(key, part):
    counts = page_counts(key)
    key = jax.random.fold_in(key, 7)
    devices = SESSIONS // SESS
    within = jax.random.randint(jax.random.fold_in(key, 1), (devices, SESS), 1, PAGE + 1, dtype=jnp.int32)
    drawn_lengths = (counts - 1) * PAGE + within
    return jnp.where(counts == PMAX, LMAX, drawn_lengths).reshape(SESSIONS).astype(jnp.int32)


def draw_query_latent(key, part):
    result = jax.random.normal(jax.random.fold_in(key, 111), (SESSIONS, HEADS, KV), jnp.float32)
    return result.astype(jnp.bfloat16)


def draw_query_rope(key, part):
    result = jax.random.normal(jax.random.fold_in(key, 112), (SESSIONS, HEADS * ROPE), jnp.float32)
    return result.astype(jnp.bfloat16)


def block_levels(key, extent, shards, smallest, largest):
    level = 1.0
    for dim, blocks in shards:
        heights = jax.random.uniform(jax.random.fold_in(jax.random.fold_in(key, 6), dim), (blocks,), jnp.float32, smallest / len(shards), largest / len(shards))
        level = level * jnp.repeat(jnp.exp(heights), extent[dim] // blocks).reshape((-1,) + (1,) * (len(extent) - 1 - dim))
    return level


def shared_out(rng, own, number, rows, number_of, top, bound, lean):
    order = jax.random.permutation(rng, number_of)
    heavy_load, usual = portions_of(number_of, rows * top, bound, lean, True), portions_of(number_of, rows * top, bound, lean, False)
    places = jnp.arange(number_of)

    def named(tallies, rotation):
        used = int((tallies > 0).sum())
        fixed = max(1, used // 4)
        moved = fixed + (places - fixed + rotation * (used - fixed)) % max(1, number_of - fixed)
        return jnp.zeros((number_of,), jnp.int32).at[order[jnp.where(places < fixed, places, moved)]].set(jnp.asarray(tallies, jnp.int32))

    tallies = jnp.where(number % 4 == 0, named(heavy_load, number // 4), named(usual, number - number // 4 - 1))
    mixed = jax.random.permutation(jax.random.fold_in(own, 3), number_of)
    giver, taker = mixed[0:number_of // 2 * 2:2], mixed[1:number_of // 2 * 2:2]
    margin = jnp.minimum(tallies[giver] - 1, bound - tallies[taker]) // 2
    margin = jnp.where((giver == order[0]) | (taker == order[0]) | (tallies[taker] == 0), 0, jnp.maximum(margin, 0))
    moved = jax.random.randint(jax.random.fold_in(own, 4), (number_of // 2,), 0, 1 << 20) % (margin + 1)
    tallies = tallies.at[giver].add(-moved).at[taker].add(moved)
    items = jnp.searchsorted(jnp.cumsum(tallies), jnp.arange(rows * top), side="right").astype(jnp.int32)
    listing = items.reshape(top, rows).T
    listing = listing[jax.random.permutation(jax.random.fold_in(own, 1), rows)]
    rotation = jax.random.randint(jax.random.fold_in(own, 2), (rows, 1), 0, top)
    return jnp.take_along_axis(listing, (jnp.arange(top)[None, :] + rotation) % top, axis=1)


def portions_of(number_of, total, reach, skew, full):
    loads = [(1 << 20) // math.isqrt(standing ** skew) + 1 for standing in range(1, number_of + 1)]
    largest = reach if full else min(reach, max(-(-total // number_of), total * loads[0] // sum(loads)))
    least = 1 if total - largest >= number_of - 1 else 0
    given, surplus = [largest] + [least] * (number_of - 1), total - largest - least * (number_of - 1)
    while surplus > 0:
        candidates = [i for i in range(1, number_of) if given[i] < largest] or [i for i in range(1, number_of) if given[i] < reach]
        pool, left = sum([loads[i] for i in candidates]), surplus
        for i in candidates:
            addition = min(reach - given[i], max(1, left * loads[i] // pool), surplus)
            given[i] = given[i] + addition
            surplus = surplus - addition
    return np.array(given)


def bell_draw(own_key, dims, scale, limit, shards=(), kind=jnp.bfloat16):
    drawn = scale * jax.random.normal(own_key, dims, jnp.float32)
    if shards:
        drawn = drawn * block_levels(own_key, dims, shards, -0.22, 0.18)
    return jnp.clip(drawn, -limit, limit).astype(kind)


def setup_inputs(seed: int = 0) -> dict:
    seeds = jax.random.split(jax.random.key(seed), 16)
    tokens = bell_draw(seeds[0], (TOKENS, D), 1.0, 6.0, ((0, 128),))
    expert_ids_keys = jax.random.split(jax.random.fold_in(seeds[1], 1), TOKENS // ROWS)
    expert_ids_turns = jax.random.permutation(jax.random.fold_in(seeds[1], 3), TOKENS // ROWS)
    expert_ids = jax.vmap(lambda own, number: shared_out(jax.random.fold_in(seeds[1], 2), own, number, ROWS, EXPERTS, TOP, CAP, 2))(expert_ids_keys, expert_ids_turns).reshape((TOKENS, TOP))
    gate_weights = jnp.clip(0.1 + 0.5 * jax.random.uniform(seeds[2], (TOKENS, TOP), jnp.float32) ** block_levels(seeds[2], (TOKENS, TOP), ((0, 128),), -0.2, 0.2), 0.1, 0.6)
    expert_gate = bell_draw(seeds[3], (EXPERTS, D, FF), D ** -0.5, 0.09375, ((0, 128),))
    expert_up = bell_draw(seeds[4], (EXPERTS, D, FF), D ** -0.5, 0.09375, ((0, 128),))
    expert_down = bell_draw(seeds[5], (EXPERTS, FF, D), FF ** -0.5, 0.1875, ((0, 128),))
    pool_latent = draw_pool_latent(jax.random.fold_in(seeds[15], 71), 0)
    pool_rope = draw_pool_rope(jax.random.fold_in(seeds[15], 71), 0)
    page_owner = draw_page_owner(jax.random.fold_in(seeds[15], 71), 0)
    page_index = draw_page_index(jax.random.fold_in(seeds[15], 71), 0)
    lengths = draw_lengths(jax.random.fold_in(seeds[15], 71), 0)
    query_latent = draw_query_latent(jax.random.fold_in(seeds[15], 71), 0)
    query_rope = draw_query_rope(jax.random.fold_in(seeds[15], 71), 0)
    new_latent = draw_new_latent(jax.random.fold_in(seeds[15], 71), 0)
    new_rope = draw_new_rope(jax.random.fold_in(seeds[15], 71), 0)
    return dict(tokens=tokens, expert_ids=expert_ids, gate_weights=gate_weights, expert_gate=expert_gate, expert_up=expert_up, expert_down=expert_down, pool_latent=pool_latent, pool_rope=pool_rope, page_owner=page_owner, page_index=page_index, lengths=lengths, query_latent=query_latent, query_rope=query_rope, new_latent=new_latent, new_rope=new_rope)


score_scale = 192.0 ** -0.5
neg_large = -1.0e30


def ranked(labels, label_count):
    onehot = (labels[..., None] == jnp.arange(label_count, dtype=jnp.int32)).astype(jnp.int32)
    before = jnp.cumsum(onehot, axis=-2) - onehot
    return jnp.sum(before * onehot, axis=-1).astype(jnp.int32)


def expert_rows(token_rows, w_gate, w_up, w_down):
    gate_proj = jnp.dot(token_rows, w_gate, preferred_element_type=jnp.float32)
    up_proj = jnp.dot(token_rows, w_up, preferred_element_type=jnp.float32)
    hidden = (jax.nn.silu(gate_proj) * up_proj).astype(jnp.bfloat16)
    return jnp.dot(hidden, w_down, preferred_element_type=jnp.float32).astype(jnp.bfloat16)


def reference(tokens, expert_ids, gate_weights, expert_gate, expert_up, expert_down, pool_latent, pool_rope, page_owner, page_index, lengths, query_latent, query_rope, new_latent, new_rope):
    blocks = TOKENS // ROWS
    pair_ids = expert_ids.reshape(blocks, ROWS * TOP).astype(jnp.int32)
    slot_ids = jnp.arange(blocks, dtype=jnp.int32)[:, None] * CAP + ranked(pair_ids, EXPERTS)
    row_ids = jnp.broadcast_to(jnp.arange(TOKENS, dtype=jnp.int32).reshape(blocks, ROWS, 1), (blocks, ROWS, TOP)).reshape(blocks, ROWS * TOP)
    slot_table = jnp.zeros((EXPERTS, blocks * CAP), jnp.int32).at[pair_ids, slot_ids].set(row_ids)

    def run_expert(packed):
        row_picks, w_gate, w_up, w_down = packed
        return expert_rows(tokens[row_picks], w_gate, w_up, w_down)

    outputs = lax.map(run_expert, (slot_table, expert_gate, expert_up, expert_down))
    picked = outputs[pair_ids, slot_ids].reshape(TOKENS, TOP, D)
    moe_out = jnp.sum(gate_weights.astype(jnp.float32)[:, :, None] * picked.astype(jnp.float32), axis=1).astype(jnp.bfloat16)

    groups = SESSIONS // SESS

    def attend_block(packed):
        owners, indices, block_lengths, block_query, block_rope, block_new, block_new_rope = packed
        pool_rows = owners * POOL + indices
        cache_latent = pool_latent[pool_rows].reshape(SESS, LMAX, KV).astype(jnp.float32)
        cache_rope = pool_rope[pool_rows].reshape(SESS, LMAX, ROPE).astype(jnp.float32)
        query_f = block_query.astype(jnp.float32)
        rope_query = block_rope.reshape(SESS, HEADS, ROPE).astype(jnp.float32)
        new_f = block_new.astype(jnp.float32)
        new_rope_f = block_new_rope.astype(jnp.float32)
        scores = jnp.einsum("shd,std->sht", query_f, cache_latent, precision=lax.Precision.HIGHEST)
        scores = scores + jnp.einsum("shr,str->sht", rope_query, cache_rope, precision=lax.Precision.HIGHEST)
        scores = scores * score_scale
        own_score = jnp.einsum("shd,sd->sh", query_f, new_f, precision=lax.Precision.HIGHEST)
        own_score = (own_score + jnp.einsum("shr,sr->sh", rope_query, new_rope_f, precision=lax.Precision.HIGHEST)) * score_scale
        positions = jnp.arange(LMAX, dtype=jnp.int32)
        visible = positions[None, None, :] < block_lengths[:, None, None]
        masked = jnp.where(visible, scores, neg_large)
        top_score = jnp.maximum(jnp.max(masked, axis=2), own_score)
        weights = jnp.where(visible, jnp.exp(masked - top_score[:, :, None]), 0.0)
        own_weight = jnp.exp(own_score - top_score)
        denominator = jnp.sum(weights, axis=2) + own_weight
        rounded = lax.optimization_barrier(weights.astype(jnp.bfloat16)).astype(jnp.float32)
        own_rounded = lax.optimization_barrier(own_weight.astype(jnp.bfloat16)).astype(jnp.float32)
        blended = jnp.einsum("sht,std->shd", rounded, cache_latent, precision=lax.Precision.HIGHEST)
        blended = blended + own_rounded[:, :, None] * new_f[:, None, :]
        return (blended / denominator[:, :, None]).astype(jnp.bfloat16)

    packed_all = (
        page_owner.reshape(groups, SESS, PMAX).astype(jnp.int32),
        page_index.reshape(groups, SESS, PMAX).astype(jnp.int32),
        lengths.reshape(groups, SESS).astype(jnp.int32),
        query_latent.reshape(groups, SESS, HEADS, KV),
        query_rope.reshape(groups, SESS, HEADS * ROPE),
        new_latent.reshape(groups, SESS, KV),
        new_rope.reshape(groups, SESS, ROPE),
    )
    attn_latent = lax.map(attend_block, packed_all).reshape(SESSIONS, HEADS, KV)
    return moe_out, attn_latent
```

```python
import jax
import jax.numpy as jnp
from jax import lax
from jax.experimental import pallas as pl
from jax.experimental.pallas import tpu as pltpu
from jax.sharding import PartitionSpec as P

MESH = pl.DeviceIdType.MESH
score_scale = 192.0 ** (-0.5)
neg_large = -1e30

DEVS = 128
MEMBERS = 32
ROWS = 32
TOP = 8
CAP = 4
D = 3584
FF = 1024
PARTS = 4
QW = D // PARTS
SLOT = CAP * PARTS
SESS = 16
HEADS = 64
KV = 512
ROPE = 64
PAGE = 64
PMAX = 16
HALF = PAGE // 2
FC = 256
NT = (((1,), (1,)), ((), ()))


def f32_dot(a, b):
    return jnp.dot(a, b, preferred_element_type=jnp.float32)


def f32_dot_nt(a, b):
    return lax.dot_general(a, b, NT, preferred_element_type=jnp.float32)


def iota(shape, dim):
    return lax.broadcasted_iota(jnp.int32, shape, dim)


def partner(g, d, k):
    core, z, x = lax.rem(d, 2), lax.rem(d // 2, 4), d // 8
    a, b, c, dc = lax.rem(k, 4), lax.rem(k // 4, 4), lax.rem(k // 16, 4), k // 64
    dx = lax.rem(a + 2 * core, 4)
    dy = lax.rem(dx + lax.rem(b + core, 4) + 1, 4)
    dz = lax.rem(dx + lax.rem(c + 3 * core, 4) + 2, 4)
    tg = lax.rem(g + dy, 4)
    td = lax.rem(x + dx, 4) * 8 + lax.rem(z + dz, 4) * 2 + lax.rem(core + dc, 2)
    return tg, td


def step_kernel(
    tokens, ids, gates, req, pool_lat, pool_rope, owner_sm, len_sm, ql, qr, nl, nr,
    wg, wu, wd,
    moe, attn,
    req_in, req_sm, tok_split, disp_out, disp_in, xrows, yrows, ret_in, hidden, ghi, glo,
    lat_send, lat_recv, rope_send, rope_recv, wgb, wub, wdb, ks, rs, nlf, nrf,
    send_sem, recv_sem, self_sem, up_sem, down_sem, sm_sem,
):
    g = lax.axis_index("grp")
    d = lax.axis_index("dev")
    me = g * MEMBERS + d

    barrier = pltpu.get_barrier_semaphore()

    def greet(k, c):
        t = lax.rem(me + k, DEVS)
        pl.semaphore_signal(
            barrier, inc=1, device_id=(t // MEMBERS, lax.rem(t, MEMBERS)), device_id_type=MESH
        )
        return c

    lax.fori_loop(1, DEVS, greet, 0)

    def up_copies(c, slot):
        cols = pl.ds(pl.multiple_of(c * FC, FC), FC)
        return (
            pltpu.make_async_copy(wg.at[0, :, cols], wgb.at[slot], up_sem.at[slot, 0]),
            pltpu.make_async_copy(wu.at[0, :, cols], wub.at[slot], up_sem.at[slot, 1]),
        )

    def down_copy(q, slot):
        cols = pl.ds(pl.multiple_of(q * QW, 128), QW)
        return pltpu.make_async_copy(wd.at[0, :, cols], wdb.at[slot], down_sem.at[slot])

    for slot in range(2):
        for copy in up_copies(slot, slot):
            copy.start()
        down_copy(slot, slot).start()

    lane = iota((ROWS, DEVS), 1)
    named = jnp.zeros((ROWS, DEVS), jnp.float32)
    weight = jnp.zeros((ROWS, DEVS), jnp.float32)
    for k in range(TOP):
        hit = ids[:, k : k + 1] == lane
        named = named + jnp.where(hit, 1.0, 0.0)
        weight = weight + jnp.where(hit, gates[:, k : k + 1], 0.0)
    earlier = jnp.where(iota((ROWS, ROWS), 0) > iota((ROWS, ROWS), 1), 1.0, 0.0)
    rank = f32_dot(earlier.astype(jnp.bfloat16), named.astype(jnp.bfloat16))
    place = (named * (rank + 1.0)).astype(jnp.bfloat16)
    place4 = jnp.concatenate([place] * PARTS, axis=0)
    w_hi = weight.astype(jnp.bfloat16)
    w_lo = (weight - w_hi.astype(jnp.float32)).astype(jnp.bfloat16)
    whi4 = jnp.concatenate([w_hi] * PARTS, axis=0)
    wlo4 = jnp.concatenate([w_lo] * PARTS, axis=0)
    for q in range(PARTS):
        tok_split[q * ROWS : (q + 1) * ROWS, :] = tokens[:, q * QW : (q + 1) * QW]

    BLK = 256

    def build(b, c):
        spread = jnp.where(
            iota((BLK, DEVS), 1) == b * (BLK // SLOT) + iota((BLK, DEVS), 0) // SLOT, 1.0, 0.0
        ).astype(jnp.bfloat16)
        row = iota((BLK, DEVS), 0)
        at = f32_dot_nt(spread, place4)
        want = (lax.rem(row // PARTS, CAP) + 1).astype(jnp.float32)
        same = lax.rem(row, PARTS) == iota((BLK, DEVS), 1) // ROWS
        pick = jnp.where((at == want) & same, 1.0, 0.0).astype(jnp.bfloat16)
        rows = pl.ds(pl.multiple_of(b * BLK, BLK), BLK)
        disp_out[rows, :] = f32_dot(pick, tok_split[...]).astype(jnp.bfloat16)
        return c

    lax.fori_loop(0, DEVS * SLOT // BLK, build, 0)

    pl.semaphore_wait(barrier, DEVS - 1)

    def slot_rows(t):
        return pl.ds(pl.multiple_of(t * SLOT, SLOT), SLOT)

    def exchange(index, src, dst, tg, td):
        t = tg * MEMBERS + td

        @pl.when(t != me)
        def _():
            pltpu.make_async_remote_copy(
                src_ref=src(t), dst_ref=dst(me), send_sem=send_sem.at[index],
                recv_sem=recv_sem.at[index], device_id=(tg, td), device_id_type=MESH,
            ).start()

        @pl.when(t == me)
        def _():
            pltpu.make_async_copy(src(me), dst(me), self_sem.at[index]).start()

    def arrived(index, rest, one):
        pltpu.make_async_copy(rest, rest, recv_sem.at[index]).wait()
        pltpu.make_async_copy(one, one, self_sem.at[index]).wait()

    def left(index, rest):
        pltpu.make_async_copy(rest, rest, send_sem.at[index]).wait()

    def send_req(k, c):
        tg, td = partner(g, d, k)
        exchange(0, lambda t: req, lambda t: req_in.at[t], tg, td)
        return c

    lax.fori_loop(0, DEVS, send_req, 0)

    def send_disp(k, c):
        tg, td = partner(g, d, k)
        exchange(
            1, lambda t: disp_out.at[slot_rows(t)], lambda t: disp_in.at[slot_rows(t)], tg, td
        )
        return c

    lax.fori_loop(0, DEVS, send_disp, 0)

    arrived(0, req_in.at[pl.ds(0, DEVS - 1)], req_in.at[0])
    to_sm = pltpu.make_async_copy(req_in, req_sm, sm_sem)
    to_sm.start()
    to_sm.wait()

    def send_page(k, c):
        tg, td = partner(g, d, k)
        t = tg * MEMBERS + td
        index = req_sm[t, 0, me]
        lat_send[t] = pool_lat[index]
        rope_send[t] = pool_rope[index]
        exchange(2, lambda t: lat_send.at[t], lambda t: lat_recv.at[t], tg, td)
        exchange(3, lambda t: rope_send.at[t], lambda t: rope_recv.at[t], tg, td)
        return c

    lax.fori_loop(0, DEVS, send_page, 0)

    def build_gates(b, c):
        spread = jnp.where(
            iota((BLK, DEVS), 1) == b * (BLK // SLOT) + iota((BLK, DEVS), 0) // SLOT, 1.0, 0.0
        ).astype(jnp.bfloat16)
        col = iota((DEVS, BLK), 1)
        at = f32_dot_nt(place4, spread)
        want = (lax.rem(col // PARTS, CAP) + 1).astype(jnp.float32)
        keep = (at == want) & (lax.rem(col, PARTS) == iota((DEVS, BLK), 0) // ROWS)
        ghi[b] = jnp.where(keep, f32_dot_nt(whi4, spread), 0.0).astype(jnp.bfloat16)
        glo[b] = jnp.where(keep, f32_dot_nt(wlo4, spread), 0.0).astype(jnp.bfloat16)
        return c

    lax.fori_loop(0, DEVS * SLOT // BLK, build_gates, 0)

    nlf[...] = nl[...].astype(jnp.float32)
    nrf[...] = nr[...].astype(jnp.float32)

    arrived(1, disp_in.at[pl.ds(0, (DEVS - 1) * SLOT)], disp_in.at[pl.ds(0, SLOT)])
    GRP = BLK // PARTS
    major = iota((BLK, BLK), 0)
    minor = iota((BLK, BLK), 1)
    apart = jnp.where(
        minor == lax.rem(major, GRP) * PARTS + major // GRP, 1.0, 0.0
    ).astype(jnp.bfloat16)
    together = jnp.where(
        major == lax.rem(minor, GRP) * PARTS + minor // GRP, 1.0, 0.0
    ).astype(jnp.bfloat16)

    def gather_rows(b, c):
        rows = pl.ds(pl.multiple_of(b * BLK, BLK), BLK)
        block = f32_dot(apart, disp_in[rows, :]).astype(jnp.bfloat16)
        for q in range(PARTS):
            xrows[pl.ds(pl.multiple_of(b * GRP, GRP), GRP), q * QW : (q + 1) * QW] = block[
                q * GRP : (q + 1) * GRP
            ]
        return c

    lax.fori_loop(0, DEVS * SLOT // BLK, gather_rows, 0)

    def up(c, carry):
        slot = lax.rem(c, 2)
        for copy in up_copies(c, slot):
            copy.wait()
        gate_proj = f32_dot(xrows[...], wgb[slot])
        up_proj = f32_dot(xrows[...], wub[slot])
        hidden[c] = (gate_proj / (1.0 + jnp.exp(-gate_proj)) * up_proj).astype(jnp.bfloat16)

        @pl.when(c + 2 < FF // FC)
        def _():
            for copy in up_copies(c + 2, slot):
                copy.start()

        return carry

    lax.fori_loop(0, FF // FC, up, 0)

    def down(q, carry):
        slot = lax.rem(q, 2)
        down_copy(q, slot).wait()
        total = f32_dot(hidden[0], wdb[slot, 0:FC, :])
        for c in range(1, FF // FC):
            total = total + f32_dot(hidden[c], wdb[slot, c * FC : (c + 1) * FC, :])
        total = total.astype(jnp.bfloat16)
        for b in range(DEVS * SLOT // BLK):
            disp_in[pl.ds(pl.multiple_of(b * BLK + q * GRP, GRP), GRP), :] = total[
                b * GRP : (b + 1) * GRP
            ]

        @pl.when(q + 2 < PARTS)
        def _():
            down_copy(q + 2, slot).start()

        return carry

    lax.fori_loop(0, PARTS, down, 0)

    def scatter_rows(b, c):
        rows = pl.ds(pl.multiple_of(b * BLK, BLK), BLK)
        yrows[rows, :] = f32_dot(together, disp_in[rows, :]).astype(jnp.bfloat16)
        return c

    lax.fori_loop(0, DEVS * SLOT // BLK, scatter_rows, 0)

    def send_ret(k, c):
        tg, td = partner(g, d, k)
        exchange(4, lambda t: yrows.at[slot_rows(t)], lambda t: ret_in.at[slot_rows(t)], tg, td)
        return c

    lax.fori_loop(0, DEVS, send_ret, 0)

    arrived(2, lat_recv.at[pl.ds(0, DEVS - 1)], lat_recv.at[0])
    arrived(3, rope_recv.at[pl.ds(0, DEVS - 1)], rope_recv.at[0])
    LM = PMAX * PAGE

    def session(s, c):
        for p in range(PMAX):
            owner = owner_sm[s, p]
            page = lat_recv[owner]
            ks[p * HALF : (p + 1) * HALF, :] = page[:HALF]
            ks[LM // 2 + p * HALF : LM // 2 + (p + 1) * HALF, :] = page[HALF:]
            rs[p * HALF : (p + 1) * HALF, :] = rope_recv[owner]
        q = ql[s]
        qd = qr[s]
        first = iota((HEADS, 2 * ROPE), 1) < ROPE
        zero = jnp.zeros_like(qd)
        keys = rs[...]
        rope_scores = jnp.concatenate(
            [
                f32_dot_nt(jnp.where(first, qd, zero), keys),
                f32_dot_nt(jnp.where(first, zero, qd), keys),
            ],
            axis=1,
        )
        scores = (f32_dot_nt(q, ks[...]) + rope_scores) * score_scale
        new = nlf[pl.ds(s, 1), :]
        new_r = nrf[pl.ds(s, 1), :]
        own = jnp.sum(q.astype(jnp.float32) * new, axis=1, keepdims=True)
        own = own + jnp.sum(qd[:, :ROPE].astype(jnp.float32) * new_r, axis=1, keepdims=True)
        own = own * score_scale
        at = iota((HEADS, LM), 1)
        rest = lax.rem(at, LM // 2)
        position = rest // HALF * PAGE + at // (LM // 2) * HALF + lax.rem(rest, HALF)
        visible = position < len_sm[s]
        masked = jnp.where(visible, scores, neg_large)
        top = jnp.maximum(jnp.max(masked, axis=1, keepdims=True), own)
        weights = jnp.where(visible, jnp.exp(masked - top), 0.0)
        own_weight = jnp.exp(own - top)
        denominator = jnp.sum(weights, axis=1, keepdims=True) + own_weight
        blended = f32_dot(weights.astype(jnp.bfloat16), ks[...])
        blended = blended + own_weight.astype(jnp.bfloat16).astype(jnp.float32) * new
        attn[s] = (blended / denominator).astype(jnp.bfloat16)
        return c

    lax.fori_loop(0, SESS, session, 0)

    arrived(4, ret_in.at[pl.ds(0, (DEVS - 1) * SLOT)], ret_in.at[pl.ds(0, SLOT)])
    total = jnp.zeros((DEVS, QW), jnp.float32)
    for b in range(DEVS * SLOT // BLK):
        block = ret_in[b * BLK : (b + 1) * BLK, :]
        total = total + f32_dot(ghi[b], block) + f32_dot(glo[b], block)
    for q in range(PARTS):
        moe[:, q * QW : (q + 1) * QW] = total[q * ROWS : (q + 1) * ROWS].astype(jnp.bfloat16)

    left(0, req_in.at[pl.ds(0, DEVS - 1)])
    left(1, disp_out.at[pl.ds(0, (DEVS - 1) * SLOT)])
    left(2, lat_send.at[pl.ds(0, DEVS - 1)])
    left(3, rope_send.at[pl.ds(0, DEVS - 1)])
    left(4, yrows.at[pl.ds(0, (DEVS - 1) * SLOT)])


def on_device(
    tokens, expert_ids, gate_weights, expert_gate, expert_up, expert_down, pool_latent, pool_rope,
    page_owner, page_index, lengths, query_latent, query_rope, new_latent, new_rope,
):
    slot = jnp.arange(PMAX, dtype=jnp.int32)
    in_use = slot[None, :] * PAGE < lengths[:, None]
    asked = jnp.where(in_use, page_owner, -1).reshape(-1)
    device = jnp.arange(DEVS, dtype=jnp.int32)
    req = jnp.sum(
        jnp.where(asked[:, None] == device[None, :], page_index.reshape(-1)[:, None], 0), axis=0
    ).astype(jnp.int32)[None, :]
    rope_pages = (
        pool_rope.reshape(-1, 2, HALF, ROPE).transpose(0, 2, 1, 3).reshape(-1, HALF, 2 * ROPE)
    )
    rope_query = query_rope.reshape(SESS, HEADS, ROPE)
    rope_query = jnp.concatenate([rope_query, rope_query], axis=2)
    vmem = pl.BlockSpec(memory_space=pltpu.VMEM)
    smem = pl.BlockSpec(memory_space=pltpu.SMEM)
    hbm = pl.BlockSpec(memory_space=pl.ANY)
    bf = jnp.bfloat16
    slots = DEVS * SLOT
    return pl.pallas_call(
        step_kernel,
        out_shape=(
            jax.ShapeDtypeStruct((ROWS, D), bf),
            jax.ShapeDtypeStruct((SESS, HEADS, KV), bf),
        ),
        in_specs=[vmem] * 6 + [smem] * 2 + [vmem] * 4 + [hbm] * 3,
        out_specs=(vmem, vmem),
        scratch_shapes=[
            pltpu.VMEM((DEVS, 1, DEVS), jnp.int32),
            pltpu.SMEM((DEVS, 1, DEVS), jnp.int32),
            pltpu.VMEM((PARTS * ROWS, QW), bf),
            pltpu.VMEM((slots, QW), bf),
            pltpu.VMEM((slots, QW), bf),
            pltpu.VMEM((DEVS * CAP, D), bf),
            pltpu.VMEM((slots, QW), bf),
            pltpu.VMEM((slots, QW), bf),
            pltpu.VMEM((FF // FC, DEVS * CAP, FC), bf),
            pltpu.VMEM((slots // 256, DEVS, 256), bf),
            pltpu.VMEM((slots // 256, DEVS, 256), bf),
            pltpu.VMEM((DEVS, PAGE, KV), bf),
            pltpu.VMEM((DEVS, PAGE, KV), bf),
            pltpu.VMEM((DEVS, HALF, 2 * ROPE), bf),
            pltpu.VMEM((DEVS, HALF, 2 * ROPE), bf),
            pltpu.VMEM((2, D, FC), bf),
            pltpu.VMEM((2, D, FC), bf),
            pltpu.VMEM((2, FF, QW), bf),
            pltpu.VMEM((PMAX * PAGE, KV), bf),
            pltpu.VMEM((PMAX * HALF, 2 * ROPE), bf),
            pltpu.VMEM((SESS, KV), jnp.float32),
            pltpu.VMEM((SESS, ROPE), jnp.float32),
            pltpu.SemaphoreType.DMA((5,)),
            pltpu.SemaphoreType.DMA((5,)),
            pltpu.SemaphoreType.DMA((5,)),
            pltpu.SemaphoreType.DMA((2, 2)),
            pltpu.SemaphoreType.DMA((2,)),
            pltpu.SemaphoreType.DMA,
        ],
        compiler_params=pltpu.CompilerParams(
            collective_id=0, has_side_effects=True, vmem_limit_bytes=62 * 2**20
        ),
    )(
        tokens, expert_ids, gate_weights, req, pool_latent, rope_pages, page_owner, lengths,
        query_latent, rope_query, new_latent, new_rope, expert_gate, expert_up, expert_down,
    )


def solution(mesh):
    both = ("grp", "dev")
    in_specs = (
        P(both, None), P(both, None), P(both, None), P(both, None, None), P(both, None, None),
        P(both, None, None), P(both, None, None), P(both, None), P(both, None), P(both, None),
        P(both), P(both, None, None), P(both, None), P(both, None), P(both, None),
    )
    out_specs = (P(both, None), P(both, None, None))
    return jax.shard_map(
        on_device, mesh=mesh, in_specs=in_specs, out_specs=out_specs, check_vma=False
    )
```

```python
import jax
import jax.numpy as jnp
from jax import lax
from jax.experimental import pallas as pl
from jax.experimental.pallas import tpu as pltpu
from jax.sharding import PartitionSpec as P

MESH = pl.DeviceIdType.MESH
score_scale = 192.0 ** (-0.5)
neg_large = -1e30

DEVS = 128
MEMBERS = 32
ROWS = 32
TOP = 8
CAP = 4
D = 3584
FF = 1024
SESS = 16
HEADS = 64
KV = 512
ROPE = 64
PAGE = 64
PMAX = 16
HALF = PAGE // 2
FC = 256
WIDTH = (1280, 1152, 1152)
START = (0, 1280, 2432)
AXES = 3
LINE = 4
PLANE = DEVS // LINE
SLOT = LINE * CAP
SLOTS = PLANE * SLOT
BLK = 256
EARLY = 8
NEAR = 8
REQ, LAT, ROP, META, AG, DISP, RET, PART = 0, 2, 3, 4, 5, 8, 11, 14
NT = (((1,), (1,)), ((), ()))


def f32_dot(a, b):
    return jnp.dot(a, b, preferred_element_type=jnp.float32)


def f32_dot_nt(a, b):
    return lax.dot_general(a, b, NT, preferred_element_type=jnp.float32)


def iota(shape, dim):
    return lax.broadcasted_iota(jnp.int32, shape, dim)


def ones_where(mask):
    return jnp.where(mask, 1.0, 0.0).astype(jnp.bfloat16)


def partner(g, d, k):
    core, z, x = lax.rem(d, 2), lax.rem(d // 2, 4), d // 8
    a, b, c, dc = lax.rem(k, 4), lax.rem(k // 4, 4), lax.rem(k // 16, 4), k // 64
    dx = lax.rem(a + 2 * core, 4)
    dy = lax.rem(dx + lax.rem(b + core, 4) + 1, 4)
    dz = lax.rem(dx + lax.rem(c + 3 * core, 4) + 2, 4)
    tg = lax.rem(g + dy, 4)
    td = lax.rem(x + dx, 4) * 8 + lax.rem(z + dz, 4) * 2 + lax.rem(core + dc, 2)
    return tg * MEMBERS + td


def plane_partner(a, b, core, k):
    da = lax.rem(k, 4) + 2 * core
    ta = lax.rem(a + da, 4)
    tb = lax.rem(b + da + lax.rem(k // 4, 4) + 1 + core, 4)
    return ta * 8 + tb * 2 + lax.rem(core + k // 16, 2)


def device_of(f, u, m):
    if f == 0:
        return u // 8 * 32 + m * 8 + lax.rem(u, 8)
    if f == 1:
        return m * 32 + u
    return u // 8 * 32 + lax.rem(u, 8) // 2 * 8 + m * 2 + lax.rem(u, 2)


def unfold(tiles, index):
    pairs = tiles[pl.ds(index, HEADS // 2, stride=SESS), :].astype(jnp.bfloat16)
    twice = f32_dot(
        ones_where(iota((HEADS, HEADS // 2), 0) // 2 == iota((HEADS, HEADS // 2), 1)), pairs
    )
    mine = iota((HEADS, 2 * ROPE), 1) // ROPE == lax.rem(iota((HEADS, 2 * ROPE), 0), 2)
    half = jnp.where(mine, twice, 0.0)
    return half + pltpu.roll(half, ROPE, 1)


def step_kernel(
    tokens, ids, gates, pool_lat, pool_rope, owner_sm, index_sm, len_sm, ql, qr, nl, nr,
    wg, wu, wd,
    moe, attn,
    req_in, req_sm, meta_out, meta_in,
    ag0, ag1, ag2, out0, out1, out2, in0, in1, in2, ret0, ret1, ret2,
    po0, po1, po2, pi0, pi1, pi2, gg, placed, weighed, xrows, hidden,
    lat_send, lat_recv, rope_pack, rope_send, rope_recv, wgb, wub, wdb, ks, rs, nlf, nrf,
    qtiles, ptiles,
    send_sem, recv_sem, self_sem, up_sem, down_sem, sm_sem,
):
    ag, disp_out, disp_in, ret_in = (ag0, ag1, ag2), (out0, out1, out2), (in0, in1, in2), (
        ret0, ret1, ret2,
    )
    part_out, part_in = (po0, po1, po2), (pi0, pi1, pi2)
    g = lax.axis_index("grp")
    d = lax.axis_index("dev")
    me = g * MEMBERS + d
    core, z, x = lax.rem(d, 2), lax.rem(d // 2, 4), d // 8
    across = ((g, z), (x, z), (g, x))
    along = (x, g, z)
    place = tuple(a * 8 + b * 2 + core for a, b in across)

    barrier = pltpu.get_barrier_semaphore()

    def greet(k, c):
        t = lax.rem(me + k, DEVS)
        pl.semaphore_signal(
            barrier, inc=1, device_id=(t // MEMBERS, lax.rem(t, MEMBERS)), device_id_type=MESH
        )
        return c

    lax.fori_loop(1, DEVS, greet, 0)

    def up_copies(c, slot):
        cols = pl.ds(pl.multiple_of(c * FC, FC), FC)
        return (
            pltpu.make_async_copy(wg.at[0, :, cols], wgb.at[slot], up_sem.at[slot, 0]),
            pltpu.make_async_copy(wu.at[0, :, cols], wub.at[slot], up_sem.at[slot, 1]),
        )

    def down_copy(f):
        slot = f % 2
        return pltpu.make_async_copy(
            wd.at[0, :, pl.ds(START[f], WIDTH[f])],
            wdb.at[slot, :, pl.ds(0, WIDTH[f])],
            down_sem.at[slot],
        )

    for slot in range(2):
        for copy in up_copies(slot, slot):
            copy.start()
        down_copy(slot).start()

    lane = iota((1, DEVS), 1)

    def ask(s, asked):
        for p in range(PMAX):
            owner = jnp.where(p * PAGE < len_sm[s], owner_sm[s, p], -1)
            asked = jnp.where(lane == owner, index_sm[s, p], asked)
        return asked

    req_in[me] = lax.fori_loop(0, SESS, ask, jnp.zeros((1, DEVS), jnp.int32))

    choice = jnp.concatenate([ids[...].astype(jnp.float32), gates[...]], axis=0)
    choice = jnp.concatenate([choice] * LINE, axis=1)
    own_lanes = iota((2 * TOP, DEVS), 1) // ROWS
    for f in range(AXES):
        mine = jnp.where(own_lanes == along[f], choice, 0.0)
        meta_out[f] = mine
        meta_in[f * LINE + along[f]] = mine
        ag[f][pl.ds(pl.multiple_of(along[f] * ROWS, ROWS), ROWS), :] = tokens[
            :, START[f] : START[f] + WIDTH[f]
        ]

    for j in range(HEADS // 2):
        cols = slice(j * 2 * ROPE, (j + 1) * 2 * ROPE)
        ptiles[j * SESS : (j + 1) * SESS, :] = pool_rope[:, cols].astype(jnp.float32)
        qtiles[j * SESS : (j + 1) * SESS, :] = qr[:, cols].astype(jnp.float32)

    def pack(page, c):
        both = unfold(ptiles, page)
        first = iota((HALF, 2 * ROPE), 1) < ROPE
        rope_pack[page] = jnp.where(first, both[:HALF], both[HALF:]).astype(jnp.bfloat16)
        return c

    lax.fori_loop(0, SESS, pack, 0)
    nlf[...] = nl[...].astype(jnp.float32)
    nrf[...] = nr[...].astype(jnp.float32)

    pl.semaphore_wait(barrier, DEVS - 1)

    def send(index, src, dst, t):
        pltpu.make_async_remote_copy(
            src_ref=src, dst_ref=dst, send_sem=send_sem.at[index], recv_sem=recv_sem.at[index],
            device_id=(t // MEMBERS, lax.rem(t, MEMBERS)), device_id_type=MESH,
        ).start()

    def exchange(index, src, dst, t):
        @pl.when(t != me)
        def _():
            send(index, src, dst, t)

        @pl.when(t == me)
        def _():
            pltpu.make_async_copy(src, dst, self_sem.at[index]).start()

    def arrived(index, others, own=None):
        pltpu.make_async_copy(others, others, recv_sem.at[index]).wait()
        if own is not None:
            pltpu.make_async_copy(own, own, self_sem.at[index]).wait()

    def left(index, others):
        pltpu.make_async_copy(others, others, send_sem.at[index]).wait()

    def rows_of(t, size):
        return pl.ds(pl.multiple_of(t * size, size), size)

    near, far = lax.rem(me, NEAR), me // NEAR
    for h in range(1, NEAR):
        row = req_in.at[me]
        send(REQ, row, row, far * NEAR + lax.rem(near + h, NEAR))
    for h in range(1, LINE):
        for f in range(AXES):
            t = device_of(f, place[f], lax.rem(along[f] + h, LINE))
            send(META, meta_out.at[f], meta_in.at[f * LINE + along[f]], t)
    for h in range(1, LINE):
        for f in range(AXES):
            t = device_of(f, place[f], lax.rem(along[f] + h, LINE))
            block = ag[f].at[rows_of(along[f], ROWS)]
            send(AG + f, block, block, t)

    arrived(REQ, req_in.at[pl.ds(0, NEAR - 1)])

    def send_req(h, c):
        rows = req_in.at[rows_of(far, NEAR)]
        send(REQ + 1, rows, rows, lax.rem(far + h, DEVS // NEAR) * NEAR + near)
        return c

    lax.fori_loop(1, DEVS // NEAR, send_req, 0)
    arrived(REQ + 1, req_in.at[pl.ds(0, DEVS - NEAR)])
    to_sm = pltpu.make_async_copy(req_in, req_sm, sm_sem)
    to_sm.start()
    to_sm.wait()

    def send_page(k, c):
        t = partner(g, d, k)
        index = req_sm[t, 0, me]
        lat_send[t] = pool_lat[index]
        rope_send[t] = rope_pack[index]
        exchange(LAT, lat_send.at[t], lat_recv.at[me], t)
        exchange(ROP, rope_send.at[t], rope_recv.at[me], t)
        return c

    lax.fori_loop(0, EARLY, send_page, 0)

    arrived(META, meta_in.at[pl.ds(0, AXES * (LINE - 1))])
    expert = iota((DEVS, DEVS), 0)
    from_row, to_row = expert, iota((DEVS, DEVS), 1)
    earlier = ones_where((from_row // ROWS == to_row // ROWS) & (from_row < to_row))
    for f in range(AXES):
        line = meta_in[f * LINE]
        for m in range(1, LINE):
            line = line + meta_in[f * LINE + m]
        chosen = line[:TOP].astype(jnp.int32)
        named = jnp.zeros((DEVS, DEVS), jnp.float32)
        weight = jnp.zeros((DEVS, DEVS), jnp.float32)
        for k in range(TOP):
            hit = chosen[k : k + 1] == expert
            named = named + jnp.where(hit, 1.0, 0.0)
            weight = weight + jnp.where(hit, line[TOP + k : TOP + k + 1], 0.0)
        rank = f32_dot(named.astype(jnp.bfloat16), earlier)
        placed[f] = named * (rank + 1.0)
        weighed[f] = weight

    for f in range(AXES):
        arrived(AG + f, ag[f].at[pl.ds(0, (LINE - 1) * ROWS)])
        for b in range(SLOTS // BLK):
            row = iota((BLK, DEVS), 0) + b * BLK
            col = iota((BLK, DEVS), 1)
            spread = ones_where(col == device_of(f, row // SLOT, along[f]))
            at = f32_dot(spread, placed[f].astype(jnp.bfloat16))
            want = (lax.rem(row, CAP) + 1).astype(jnp.float32)
            pick = ones_where((at == want) & (lax.rem(row // CAP, LINE) == col // ROWS))
            disp_out[f][b * BLK : (b + 1) * BLK, :] = f32_dot(pick, ag[f][...]).astype(
                jnp.bfloat16
            )

    def send_disp(k, c):
        for f in range(AXES):
            u = plane_partner(*across[f], core, k)
            exchange(
                DISP + f, disp_out[f].at[rows_of(u, SLOT)], disp_in[f].at[rows_of(place[f], SLOT)],
                device_of(f, u, along[f]),
            )
        return c

    lax.fori_loop(0, PLANE, send_disp, 0)
    lax.fori_loop(EARLY, DEVS, send_page, 0)

    for f in range(AXES):
        row = iota((DEVS, SLOTS), 0)
        col = iota((DEVS, SLOTS), 1)
        spread = ones_where(row == device_of(f, col // SLOT, along[f]))
        at = f32_dot(placed[f].T.astype(jnp.bfloat16), spread)
        want = (lax.rem(col, CAP) + 1).astype(jnp.float32)
        keep = (at == want) & (lax.rem(col // CAP, LINE) == row // ROWS)
        weight = weighed[f].T
        high = weight.astype(jnp.bfloat16)
        low = (weight - high.astype(jnp.float32)).astype(jnp.bfloat16)
        gg[f, 0:DEVS, :] = jnp.where(keep, f32_dot(high, spread), 0.0).astype(jnp.bfloat16)
        gg[f, DEVS:, :] = jnp.where(keep, f32_dot(low, spread), 0.0).astype(jnp.bfloat16)

    def source_row(f, at):
        return device_of(f, at // SLOT, lax.rem(at // CAP, LINE)) * CAP + lax.rem(at, CAP)

    for f in range(AXES):
        arrived(
            DISP + f, disp_in[f].at[pl.ds(0, SLOTS - SLOT)], disp_in[f].at[pl.ds(0, SLOT)]
        )
        goes_to = source_row(f, iota((1, SLOTS), 1))
        for b in range(SLOTS // BLK):
            order = ones_where(iota((BLK, SLOTS), 0) + b * BLK == goes_to)
            xrows[b * BLK : (b + 1) * BLK, START[f] : START[f] + WIDTH[f]] = f32_dot(
                order, disp_in[f][...]
            ).astype(jnp.bfloat16)

    def up(c, carry):
        slot = lax.rem(c, 2)
        for copy in up_copies(c, slot):
            copy.wait()
        gate_proj = f32_dot(xrows[...], wgb[slot])
        up_proj = f32_dot(xrows[...], wub[slot])
        hidden[c] = (gate_proj / (1.0 + jnp.exp(-gate_proj)) * up_proj).astype(jnp.bfloat16)

        @pl.when(c + 2 < FF // FC)
        def _():
            for copy in up_copies(c + 2, slot):
                copy.start()

        return carry

    lax.fori_loop(0, FF // FC, up, 0)

    for f in range(AXES):
        down_copy(f).wait()
        slot = f % 2
        total = f32_dot(hidden[0], wdb[slot, 0:FC, 0 : WIDTH[f]])
        for c in range(1, FF // FC):
            total = total + f32_dot(hidden[c], wdb[slot, c * FC : (c + 1) * FC, 0 : WIDTH[f]])
        xrows[:, START[f] : START[f] + WIDTH[f]] = total.astype(jnp.bfloat16)
        if f + 2 < AXES:
            down_copy(f + 2).start()
        for b in range(SLOTS // BLK):
            comes_from = source_row(f, iota((BLK, 1), 0) + b * BLK)
            order = ones_where(iota((BLK, SLOTS), 1) == comes_from)
            disp_in[f][b * BLK : (b + 1) * BLK, :] = f32_dot(
                order, xrows[:, START[f] : START[f] + WIDTH[f]]
            ).astype(jnp.bfloat16)

    def send_ret(k, c):
        for f in range(AXES):
            u = plane_partner(*across[f], core, k)
            exchange(
                RET + f, disp_in[f].at[rows_of(u, SLOT)], ret_in[f].at[rows_of(place[f], SLOT)],
                device_of(f, u, along[f]),
            )
        return c

    lax.fori_loop(0, PLANE, send_ret, 0)

    arrived(LAT, lat_recv.at[pl.ds(0, DEVS - 1)], lat_recv.at[0])
    arrived(ROP, rope_recv.at[pl.ds(0, DEVS - 1)], rope_recv.at[0])
    LM = PMAX * PAGE

    def session(s, c):
        for p in range(PMAX):
            owner = owner_sm[s, p]
            page = lat_recv[owner]
            ks[p * HALF : (p + 1) * HALF, :] = page[:HALF]
            ks[LM // 2 + p * HALF : LM // 2 + (p + 1) * HALF, :] = page[HALF:]
            rs[p * HALF : (p + 1) * HALF, :] = rope_recv[owner]
        q = ql[s]
        qd = unfold(qtiles, s)
        first = iota((HEADS, 2 * ROPE), 1) < ROPE
        keys = rs[...]
        rope_scores = jnp.concatenate(
            [
                f32_dot_nt(jnp.where(first, qd, 0.0).astype(jnp.bfloat16), keys),
                f32_dot_nt(jnp.where(first, 0.0, qd).astype(jnp.bfloat16), keys),
            ],
            axis=1,
        )
        scores = (f32_dot_nt(q, ks[...]) + rope_scores) * score_scale
        new = nlf[pl.ds(s, 1), :]
        new_r = nrf[pl.ds(s, 1), :]
        own = jnp.sum(q.astype(jnp.float32) * new, axis=1, keepdims=True)
        own = own + jnp.sum(qd[:, :ROPE] * new_r, axis=1, keepdims=True)
        own = own * score_scale
        at = iota((HEADS, LM), 1)
        rest = lax.rem(at, LM // 2)
        position = rest // HALF * PAGE + at // (LM // 2) * HALF + lax.rem(rest, HALF)
        visible = position < len_sm[s]
        masked = jnp.where(visible, scores, neg_large)
        top = jnp.maximum(jnp.max(masked, axis=1, keepdims=True), own)
        weights = jnp.where(visible, jnp.exp(masked - top), 0.0)
        own_weight = jnp.exp(own - top)
        denominator = jnp.sum(weights, axis=1, keepdims=True) + own_weight
        blended = f32_dot(weights.astype(jnp.bfloat16), ks[...])
        blended = blended + own_weight.astype(jnp.bfloat16).astype(jnp.float32) * new
        attn[s] = (blended / denominator).astype(jnp.bfloat16)
        return c

    lax.fori_loop(0, SESS, session, 0)

    for f in range(AXES):
        arrived(RET + f, ret_in[f].at[pl.ds(0, SLOTS - SLOT)], ret_in[f].at[pl.ds(0, SLOT)])
        both = f32_dot(gg[f], ret_in[f][...])
        part_out[f][...] = (both[:DEVS] + both[DEVS:]).astype(jnp.bfloat16)
        for h in range(LINE):
            m = lax.rem(along[f] + h, LINE)
            src = part_out[f].at[rows_of(m, ROWS)]
            dst = part_in[f].at[rows_of(along[f], ROWS)]
            if h == 0:
                pltpu.make_async_copy(src, dst, self_sem.at[PART + f]).start()
            else:
                send(PART + f, src, dst, device_of(f, place[f], m))

    for f in range(AXES):
        arrived(PART + f, part_in[f].at[pl.ds(0, (LINE - 1) * ROWS)], part_in[f].at[pl.ds(0, ROWS)])
        total = part_in[f][0:ROWS, :].astype(jnp.float32)
        for m in range(1, LINE):
            total = total + part_in[f][m * ROWS : (m + 1) * ROWS, :].astype(jnp.float32)
        moe[:, START[f] : START[f] + WIDTH[f]] = total.astype(jnp.bfloat16)

    left(REQ, req_in.at[pl.ds(0, NEAR - 1)])
    left(REQ + 1, req_in.at[pl.ds(0, DEVS - NEAR)])
    left(LAT, lat_send.at[pl.ds(0, DEVS - 1)])
    left(ROP, rope_send.at[pl.ds(0, DEVS - 1)])
    left(META, meta_in.at[pl.ds(0, AXES * (LINE - 1))])
    for f in range(AXES):
        left(AG + f, ag[f].at[pl.ds(0, (LINE - 1) * ROWS)])
        left(DISP + f, disp_out[f].at[pl.ds(0, SLOTS - SLOT)])
        left(RET + f, disp_in[f].at[pl.ds(0, SLOTS - SLOT)])
        left(PART + f, part_out[f].at[pl.ds(0, (LINE - 1) * ROWS)])


def on_device(
    tokens, expert_ids, gate_weights, expert_gate, expert_up, expert_down, pool_latent, pool_rope,
    page_owner, page_index, lengths, query_latent, query_rope, new_latent, new_rope,
):
    vmem = pl.BlockSpec(memory_space=pltpu.VMEM)
    smem = pl.BlockSpec(memory_space=pltpu.SMEM)
    hbm = pl.BlockSpec(memory_space=pl.ANY)
    bf = jnp.bfloat16
    line_rows = [pltpu.VMEM((LINE * ROWS, w), bf) for w in WIDTH]
    slot_rows = [pltpu.VMEM((SLOTS, w), bf) for w in WIDTH]
    return pl.pallas_call(
        step_kernel,
        out_shape=(
            jax.ShapeDtypeStruct((ROWS, D), bf),
            jax.ShapeDtypeStruct((SESS, HEADS, KV), bf),
        ),
        in_specs=[vmem] * 5 + [smem] * 3 + [vmem] * 4 + [hbm] * 3,
        out_specs=(vmem, vmem),
        scratch_shapes=[
            pltpu.VMEM((DEVS, 1, DEVS), jnp.int32),
            pltpu.SMEM((DEVS, 1, DEVS), jnp.int32),
            pltpu.VMEM((AXES, 2 * TOP, DEVS), jnp.float32),
            pltpu.VMEM((AXES * LINE, 2 * TOP, DEVS), jnp.float32),
            *line_rows, *slot_rows, *slot_rows, *slot_rows, *line_rows, *line_rows,
            pltpu.VMEM((AXES, 2 * DEVS, SLOTS), bf),
            pltpu.VMEM((AXES, DEVS, DEVS), jnp.float32),
            pltpu.VMEM((AXES, DEVS, DEVS), jnp.float32),
            pltpu.VMEM((SLOTS, D), bf),
            pltpu.VMEM((FF // FC, SLOTS, FC), bf),
            pltpu.VMEM((DEVS, PAGE, KV), bf),
            pltpu.VMEM((DEVS, PAGE, KV), bf),
            pltpu.VMEM((SESS, HALF, 2 * ROPE), bf),
            pltpu.VMEM((DEVS, HALF, 2 * ROPE), bf),
            pltpu.VMEM((DEVS, HALF, 2 * ROPE), bf),
            pltpu.VMEM((2, D, FC), bf),
            pltpu.VMEM((2, D, FC), bf),
            pltpu.VMEM((2, FF, WIDTH[0]), bf),
            pltpu.VMEM((PMAX * PAGE, KV), bf),
            pltpu.VMEM((PMAX * HALF, 2 * ROPE), bf),
            pltpu.VMEM((SESS, KV), jnp.float32),
            pltpu.VMEM((SESS, ROPE), jnp.float32),
            pltpu.VMEM((HEADS // 2 * SESS, 2 * ROPE), jnp.float32),
            pltpu.VMEM((HEADS // 2 * SESS, 2 * ROPE), jnp.float32),
            pltpu.SemaphoreType.DMA((PART + AXES,)),
            pltpu.SemaphoreType.DMA((PART + AXES,)),
            pltpu.SemaphoreType.DMA((PART + AXES,)),
            pltpu.SemaphoreType.DMA((2, 2)),
            pltpu.SemaphoreType.DMA((2,)),
            pltpu.SemaphoreType.DMA,
        ],
        compiler_params=pltpu.CompilerParams(
            collective_id=0, has_side_effects=True, vmem_limit_bytes=62 * 2**20
        ),
    )(
        tokens, expert_ids.T, gate_weights.T, pool_latent, pool_rope, page_owner, page_index,
        lengths, query_latent, query_rope, new_latent, new_rope, expert_gate, expert_up,
        expert_down,
    )


def solution(mesh):
    both = ("grp", "dev")
    in_specs = (
        P(both, None), P(both, None), P(both, None), P(both, None, None), P(both, None, None),
        P(both, None, None), P(both, None, None), P(both, None), P(both, None), P(both, None),
        P(both), P(both, None, None), P(both, None), P(both, None), P(both, None),
    )
    out_specs = (P(both, None), P(both, None, None))
    return jax.shard_map(
        on_device, mesh=mesh, in_specs=in_specs, out_specs=out_specs, check_vma=False
    )
```

```python
import jax
import jax.numpy as jnp
from jax import lax
from jax.experimental import pallas as pl
from jax.experimental.pallas import tpu as pltpu
from jax.sharding import PartitionSpec as P

MESH = pl.DeviceIdType.MESH
score_scale = 192.0 ** (-0.5)
neg_large = -1e30

DEVS = 128
MEMBERS = 32
ROWS = 32
TOP = 8
CAP = 4
D = 3584
FF = 1024
SESS = 16
HEADS = 64
KV = 512
ROPE = 64
PAGE = 64
PMAX = 16
HALF = PAGE // 2
FC = 256
WIDTH = (1280, 1152, 1152)
START = (0, 1280, 2432)
PAIR = 2
LATE = 256
AXES = 3
LINE = 4
PLANE = DEVS // LINE
SLOT = LINE * CAP
SLOTS = PLANE * SLOT
BLK = 256
EARLY = 8
NEAR = 8
REQ, LAT, ROP, META, AG, DISP, RET, PART = 0, 2, 3, 4, 5, 8, 11, 17
NT = (((1,), (1,)), ((), ()))


def f32_dot(a, b):
    return jnp.dot(a, b, preferred_element_type=jnp.float32)


def f32_dot_nt(a, b):
    return lax.dot_general(a, b, NT, preferred_element_type=jnp.float32)


def iota(shape, dim):
    return lax.broadcasted_iota(jnp.int32, shape, dim)


def ones_where(mask):
    return jnp.where(mask, 1.0, 0.0).astype(jnp.bfloat16)


def partner(g, d, k):
    core, z, x = lax.rem(d, 2), lax.rem(d // 2, 4), d // 8
    a, b, c, dc = lax.rem(k, 4), lax.rem(k // 4, 4), lax.rem(k // 16, 4), k // 64
    dx = lax.rem(a + 2 * core, 4)
    dy = lax.rem(dx + lax.rem(b + core, 4) + 1, 4)
    dz = lax.rem(dx + lax.rem(c + 3 * core, 4) + 2, 4)
    tg = lax.rem(g + dy, 4)
    td = lax.rem(x + dx, 4) * 8 + lax.rem(z + dz, 4) * 2 + lax.rem(core + dc, 2)
    return tg * MEMBERS + td


def plane_partner(a, b, core, k):
    da = lax.rem(k, 4) + 2 * core
    ta = lax.rem(a + da, 4)
    tb = lax.rem(b + da + lax.rem(k // 4, 4) + 1 + core, 4)
    return ta * 8 + tb * 2 + lax.rem(core + k // 16, 2)


def device_of(f, u, m):
    if f == 0:
        return u // 8 * 32 + m * 8 + lax.rem(u, 8)
    if f == 1:
        return m * 32 + u
    return u // 8 * 32 + lax.rem(u, 8) // 2 * 8 + m * 2 + lax.rem(u, 2)


def unfold(tiles, index):
    pairs = tiles[pl.ds(index, HEADS // 2, stride=SESS), :].astype(jnp.bfloat16)
    twice = f32_dot(
        ones_where(iota((HEADS, HEADS // 2), 0) // 2 == iota((HEADS, HEADS // 2), 1)), pairs
    )
    mine = iota((HEADS, 2 * ROPE), 1) // ROPE == lax.rem(iota((HEADS, 2 * ROPE), 0), 2)
    half = jnp.where(mine, twice, 0.0)
    return half + pltpu.roll(half, ROPE, 1)


def step_kernel(
    tokens, ids, gates, pool_rope, owner_sm, index_sm, len_sm, qr, nl, nr,
    pool_hbm, query_hbm, wg, wu, wd,
    moe, attn_hbm,
    pool_lat, ql, attn,
    req_in, req_sm, meta_out, meta_in,
    ag0, ag1, ag2, out0, out1, out2, in0, in1, in2, ret0, ret1, ret2,
    po0, po1, po2, pi0, pi1, pi2, gg, placed, weighed, xrows, hidden,
    lat_send, lat_recv, rope_pack, rope_send, rope_recv, wgb, wub, wdb, ks, rs, qrope, owns, nlf, nrf,
    qtiles, ptiles,
    send_sem, recv_sem, self_sem, up_sem, down_sem, sm_sem, pool_sem, query_sem, attn_sem,
):
    ag, disp_out, disp_in, ret_in = (ag0, ag1, ag2), (out0, out1, out2), (in0, in1, in2), (
        ret0, ret1, ret2,
    )
    part_out, part_in = (po0, po1, po2), (pi0, pi1, pi2)
    g = lax.axis_index("grp")
    d = lax.axis_index("dev")
    me = g * MEMBERS + d
    core, z, x = lax.rem(d, 2), lax.rem(d // 2, 4), d // 8
    across = ((g, z), (x, z), (g, x))
    along = (x, g, z)
    place = tuple(a * 8 + b * 2 + core for a, b in across)

    barrier = pltpu.get_barrier_semaphore()

    def greet(k, c):
        t = lax.rem(me + k, DEVS)
        pl.semaphore_signal(
            barrier, inc=1, device_id=(t // MEMBERS, lax.rem(t, MEMBERS)), device_id_type=MESH
        )
        return c

    lax.fori_loop(1, DEVS, greet, 0)

    pool_copy = pltpu.make_async_copy(pool_hbm, pool_lat, pool_sem)
    pool_copy.start()
    query_copy = pltpu.make_async_copy(query_hbm, ql, query_sem)
    query_copy.start()

    def up_copies(c, slot):
        cols = pl.ds(pl.multiple_of(c * FC, FC), FC)
        return (
            pltpu.make_async_copy(wg.at[0, :, cols], wgb.at[slot], up_sem.at[slot, 0]),
            pltpu.make_async_copy(wu.at[0, :, cols], wub.at[slot], up_sem.at[slot, 1]),
        )

    def down_copy(f):
        slot = f % 2
        return pltpu.make_async_copy(
            wd.at[0, :, pl.ds(START[f], WIDTH[f])],
            wdb.at[slot, :, pl.ds(0, WIDTH[f])],
            down_sem.at[slot],
        )

    for slot in range(2):
        for copy in up_copies(slot, slot):
            copy.start()
        down_copy(slot).start()

    lane = iota((1, DEVS), 1)

    def ask(s, asked):
        for p in range(PMAX):
            owner = jnp.where(p * PAGE < len_sm[s], owner_sm[s, p], -1)
            asked = jnp.where(lane == owner, index_sm[s, p], asked)
        return asked

    req_in[me] = lax.fori_loop(0, SESS, ask, jnp.zeros((1, DEVS), jnp.int32))

    choice = jnp.concatenate([ids[...].astype(jnp.float32), gates[...]], axis=0)
    choice = jnp.concatenate([choice] * LINE, axis=1)
    own_lanes = iota((2 * TOP, DEVS), 1) // ROWS
    for f in range(AXES):
        mine = jnp.where(own_lanes == along[f], choice, 0.0)
        meta_out[f] = mine
        meta_in[f * LINE + along[f]] = mine
        ag[f][pl.ds(pl.multiple_of(along[f] * ROWS, ROWS), ROWS), :] = tokens[
            :, START[f] : START[f] + WIDTH[f]
        ]

    for j in range(HEADS // 2):
        cols = slice(j * 2 * ROPE, (j + 1) * 2 * ROPE)
        ptiles[j * SESS : (j + 1) * SESS, :] = pool_rope[:, cols].astype(jnp.float32)
        qtiles[j * SESS : (j + 1) * SESS, :] = qr[:, cols].astype(jnp.float32)

    def pack(page, c):
        both = unfold(ptiles, page)
        first = iota((HALF, 2 * ROPE), 1) < ROPE
        rope_pack[page] = jnp.where(first, both[:HALF], both[HALF:]).astype(jnp.bfloat16)
        return c

    lax.fori_loop(0, SESS, pack, 0)
    nlf[...] = nl[...].astype(jnp.float32)
    nrf[...] = nr[...].astype(jnp.float32)

    pl.semaphore_wait(barrier, DEVS - 1)

    def send(index, src, dst, t):
        pltpu.make_async_remote_copy(
            src_ref=src, dst_ref=dst, send_sem=send_sem.at[index], recv_sem=recv_sem.at[index],
            device_id=(t // MEMBERS, lax.rem(t, MEMBERS)), device_id_type=MESH,
        ).start()

    def exchange(index, src, dst, t):
        @pl.when(t != me)
        def _():
            send(index, src, dst, t)

        @pl.when(t == me)
        def _():
            pltpu.make_async_copy(src, dst, self_sem.at[index]).start()

    def arrived(index, others, own=None):
        pltpu.make_async_copy(others, others, recv_sem.at[index]).wait()
        if own is not None:
            pltpu.make_async_copy(own, own, self_sem.at[index]).wait()

    def left(index, others):
        pltpu.make_async_copy(others, others, send_sem.at[index]).wait()

    def rows_of(t, size):
        return pl.ds(pl.multiple_of(t * size, size), size)

    near, far = lax.rem(me, NEAR), me // NEAR
    for h in range(1, NEAR):
        row = req_in.at[me]
        send(REQ, row, row, far * NEAR + lax.rem(near + h, NEAR))
    arrived(REQ, req_in.at[pl.ds(0, NEAR - 1)])

    def send_req(h, c):
        rows = req_in.at[rows_of(far, NEAR)]
        send(REQ + 1, rows, rows, lax.rem(far + h, DEVS // NEAR) * NEAR + near)
        return c

    lax.fori_loop(1, DEVS // NEAR, send_req, 0)
    for h in range(1, LINE):
        for f in range(AXES):
            t = device_of(f, place[f], lax.rem(along[f] + h, LINE))
            send(META, meta_out.at[f], meta_in.at[f * LINE + along[f]], t)
    for h in range(1, LINE):
        for f in range(AXES):
            t = device_of(f, place[f], lax.rem(along[f] + h, LINE))
            block = ag[f].at[rows_of(along[f], ROWS)]
            send(AG + f, block, block, t)

    arrived(REQ + 1, req_in.at[pl.ds(0, DEVS - NEAR)])
    to_sm = pltpu.make_async_copy(req_in, req_sm, sm_sem)
    to_sm.start()
    to_sm.wait()

    def send_page(k, c):
        t = partner(g, d, k)
        index = req_sm[t, 0, me]
        lat_send[t] = pool_lat[index]
        rope_send[t] = rope_pack[index]
        exchange(LAT, lat_send.at[t], lat_recv.at[me], t)
        exchange(ROP, rope_send.at[t], rope_recv.at[me], t)
        return c

    pool_copy.wait()
    lax.fori_loop(0, EARLY, send_page, 0)

    arrived(META, meta_in.at[pl.ds(0, AXES * (LINE - 1))])
    expert = iota((DEVS, DEVS), 0)
    from_row, to_row = expert, iota((DEVS, DEVS), 1)
    earlier = ones_where((from_row // ROWS == to_row // ROWS) & (from_row < to_row))
    for f in range(AXES):
        line = meta_in[f * LINE]
        for m in range(1, LINE):
            line = line + meta_in[f * LINE + m]
        chosen = line[:TOP].astype(jnp.int32)
        named = jnp.zeros((DEVS, DEVS), jnp.float32)
        weight = jnp.zeros((DEVS, DEVS), jnp.float32)
        for k in range(TOP):
            hit = chosen[k : k + 1] == expert
            named = named + jnp.where(hit, 1.0, 0.0)
            weight = weight + jnp.where(hit, line[TOP + k : TOP + k + 1], 0.0)
        rank = f32_dot(named.astype(jnp.bfloat16), earlier)
        placed[f] = named * (rank + 1.0)
        weighed[f] = weight

    for f in range(AXES):
        arrived(AG + f, ag[f].at[pl.ds(0, (LINE - 1) * ROWS)])
        for b in range(SLOTS // BLK):
            row = iota((BLK, DEVS), 0) + b * BLK
            col = iota((BLK, DEVS), 1)
            spread = ones_where(col == device_of(f, row // SLOT, along[f]))
            at = f32_dot(spread, placed[f].astype(jnp.bfloat16))
            want = (lax.rem(row, CAP) + 1).astype(jnp.float32)
            pick = ones_where((at == want) & (lax.rem(row // CAP, LINE) == col // ROWS))
            disp_out[f][b * BLK : (b + 1) * BLK, :] = f32_dot(pick, ag[f][...]).astype(
                jnp.bfloat16
            )

    def send_disp(k, c):
        for f in range(AXES):
            u = plane_partner(*across[f], core, k)
            exchange(
                DISP + f, disp_out[f].at[rows_of(u, SLOT)], disp_in[f].at[rows_of(place[f], SLOT)],
                device_of(f, u, along[f]),
            )
        return c

    lax.fori_loop(0, PLANE, send_disp, 0)
    lax.fori_loop(EARLY, DEVS, send_page, 0)

    for f in range(AXES):
        row = iota((DEVS, SLOTS), 0)
        col = iota((DEVS, SLOTS), 1)
        spread = ones_where(row == device_of(f, col // SLOT, along[f]))
        at = f32_dot(placed[f].T.astype(jnp.bfloat16), spread)
        want = (lax.rem(col, CAP) + 1).astype(jnp.float32)
        keep = (at == want) & (lax.rem(col // CAP, LINE) == row // ROWS)
        weight = weighed[f].T
        high = weight.astype(jnp.bfloat16)
        low = (weight - high.astype(jnp.float32)).astype(jnp.bfloat16)
        gg[f, 0:DEVS, :] = jnp.where(keep, f32_dot(high, spread), 0.0).astype(jnp.bfloat16)
        gg[f, DEVS:, :] = jnp.where(keep, f32_dot(low, spread), 0.0).astype(jnp.bfloat16)

    query_copy.wait()

    def prepare(s, c):
        qd = unfold(qtiles, s)
        first = iota((HEADS, 2 * ROPE), 1) < ROPE
        qrope[s, :HEADS] = jnp.where(first, qd, 0.0).astype(jnp.bfloat16)
        qrope[s, HEADS:] = jnp.where(first, 0.0, qd).astype(jnp.bfloat16)
        own = jnp.sum(ql[s].astype(jnp.float32) * nlf[pl.ds(s, 1), :], axis=1, keepdims=True)
        own = own + jnp.sum(qd[:, :ROPE] * nrf[pl.ds(s, 1), :], axis=1, keepdims=True)
        owns[s] = jnp.broadcast_to(own * score_scale, (HEADS, 2 * ROPE))
        return c

    lax.fori_loop(0, SESS, prepare, 0)

    def source_row(f, at):
        return device_of(f, at // SLOT, lax.rem(at // CAP, LINE)) * CAP + lax.rem(at, CAP)

    for f in range(AXES):
        arrived(
            DISP + f, disp_in[f].at[pl.ds(0, SLOTS - SLOT)], disp_in[f].at[pl.ds(0, SLOT)]
        )
        goes_to = source_row(f, iota((1, SLOTS), 1))
        for b in range(SLOTS // BLK):
            order = ones_where(iota((BLK, SLOTS), 0) + b * BLK == goes_to)
            xrows[b * BLK : (b + 1) * BLK, START[f] : START[f] + WIDTH[f]] = f32_dot(
                order, disp_in[f][...]
            ).astype(jnp.bfloat16)

    def up(c, carry):
        slot = lax.rem(c, 2)
        for copy in up_copies(c, slot):
            copy.wait()
        gate_proj = f32_dot(xrows[...], wgb[slot])
        up_proj = f32_dot(xrows[...], wub[slot])
        hidden[c] = (gate_proj / (1.0 + jnp.exp(-gate_proj)) * up_proj).astype(jnp.bfloat16)

        @pl.when(c + 2 < FF // FC)
        def _():
            for copy in up_copies(c + 2, slot):
                copy.start()

        return carry

    lax.fori_loop(0, FF // FC, up, 0)

    for f in range(AXES):
        down_copy(f).wait()
        slot = f % 2
        total = f32_dot(hidden[0], wdb[slot, 0:FC, 0 : WIDTH[f]])
        for c in range(1, FF // FC):
            total = total + f32_dot(hidden[c], wdb[slot, c * FC : (c + 1) * FC, 0 : WIDTH[f]])
        xrows[:, START[f] : START[f] + WIDTH[f]] = total.astype(jnp.bfloat16)
        if f + 2 < AXES:
            down_copy(f + 2).start()
        for b in range(SLOTS // BLK):
            comes_from = source_row(f, iota((BLK, 1), 0) + b * BLK)
            order = ones_where(iota((BLK, SLOTS), 1) == comes_from)
            disp_in[f][b * BLK : (b + 1) * BLK, :] = f32_dot(
                order, xrows[:, START[f] : START[f] + WIDTH[f]]
            ).astype(jnp.bfloat16)

    def columns(f, turn):
        return pl.ds(0, WIDTH[f] - LATE) if turn == 0 else pl.ds(WIDTH[f] - LATE, LATE)

    for turn in range(2):

        def send_ret(k, c, turn=turn):
            for f in range(AXES):
                u = plane_partner(*across[f], core, k)
                cols = columns(f, turn)
                exchange(
                    RET + turn * AXES + f, disp_in[f].at[rows_of(u, SLOT), cols],
                    ret_in[f].at[rows_of(place[f], SLOT), cols], device_of(f, u, along[f]),
                )
            return c

        lax.fori_loop(0, PLANE, send_ret, 0)

    arrived(LAT, lat_recv.at[pl.ds(0, DEVS - 1)], lat_recv.at[0])
    arrived(ROP, rope_recv.at[pl.ds(0, DEVS - 1)], rope_recv.at[0])
    LM = PMAX * PAGE

    def session(s, held):
        for p in range(PMAX):
            owner = owner_sm[s, p]
            page = lat_recv[owner]
            ks[held, p * HALF : (p + 1) * HALF, :] = page[:HALF]
            ks[held, LM // 2 + p * HALF : LM // 2 + (p + 1) * HALF, :] = page[HALF:]
            rs[held, p * HALF : (p + 1) * HALF, :] = rope_recv[owner]
        both = f32_dot_nt(qrope[s], rs[held])
        rope_scores = jnp.concatenate([both[:HEADS], both[HEADS:]], axis=1)
        scores = (f32_dot_nt(ql[s], ks[held]) + rope_scores) * score_scale
        own = owns[s][:, :1]
        at = iota((1, LM), 1)
        rest = lax.rem(at, LM // 2)
        position = rest // HALF * PAGE + at // (LM // 2) * HALF + lax.rem(rest, HALF)
        visible = position < len_sm[s]
        masked = jnp.where(visible, scores, neg_large)
        top = jnp.maximum(jnp.max(masked, axis=1, keepdims=True), own)
        weights = jnp.where(visible, jnp.exp(masked - top), 0.0)
        own_weight = jnp.exp(own - top)
        denominator = jnp.sum(weights, axis=1, keepdims=True) + own_weight
        blended = f32_dot(weights.astype(jnp.bfloat16), ks[held])
        own_weight = own_weight.astype(jnp.bfloat16).astype(jnp.float32)
        blended = blended + own_weight * nlf[pl.ds(s, 1), :]
        attn[s] = (blended / denominator).astype(jnp.bfloat16)

    def sessions(i, c):
        for held in range(PAIR):
            session(i * PAIR + held, held)
        return c

    lax.fori_loop(0, SESS // PAIR, sessions, 0)
    attn_copy = pltpu.make_async_copy(attn, attn_hbm, attn_sem)
    attn_copy.start()

    def add_line(f, turn):
        index = RET + turn * AXES + f
        cols = columns(f, turn)
        arrived(
            index, ret_in[f].at[pl.ds(0, SLOTS - SLOT), cols], ret_in[f].at[pl.ds(0, SLOT), cols]
        )
        both = f32_dot(gg[f], ret_in[f][:, cols])
        part_out[f][:, cols] = (both[:DEVS] + both[DEVS:]).astype(jnp.bfloat16)
        index = PART + turn * AXES + f
        for h in range(LINE):
            m = lax.rem(along[f] + h, LINE)
            src = part_out[f].at[rows_of(m, ROWS), cols]
            dst = part_in[f].at[rows_of(along[f], ROWS), cols]
            if h == 0:
                pltpu.make_async_copy(src, dst, self_sem.at[index]).start()
            else:
                send(index, src, dst, device_of(f, place[f], m))

    def add_parts(f, turn):
        cols = columns(f, turn)
        arrived(
            PART + turn * AXES + f, part_in[f].at[pl.ds(0, (LINE - 1) * ROWS), cols],
            part_in[f].at[pl.ds(0, ROWS), cols],
        )
        total = part_in[f][0:ROWS, cols].astype(jnp.float32)
        for m in range(1, LINE):
            total = total + part_in[f][m * ROWS : (m + 1) * ROWS, cols].astype(jnp.float32)
        moe[:, pl.ds(START[f] + cols.start, cols.size)] = total.astype(jnp.bfloat16)

    for turn in range(2):
        for f in range(AXES):
            add_line(f, turn)
    for turn in range(2):
        for f in range(AXES):
            add_parts(f, turn)

    attn_copy.wait()
    left(REQ, req_in.at[pl.ds(0, NEAR - 1)])
    left(REQ + 1, req_in.at[pl.ds(0, DEVS - NEAR)])
    left(LAT, lat_send.at[pl.ds(0, DEVS - 1)])
    left(ROP, rope_send.at[pl.ds(0, DEVS - 1)])
    left(META, meta_in.at[pl.ds(0, AXES * (LINE - 1))])
    for f in range(AXES):
        left(AG + f, ag[f].at[pl.ds(0, (LINE - 1) * ROWS)])
        left(DISP + f, disp_out[f].at[pl.ds(0, SLOTS - SLOT)])
        for turn in range(2):
            cols = columns(f, turn)
            left(RET + turn * AXES + f, disp_in[f].at[pl.ds(0, SLOTS - SLOT), cols])
            left(PART + turn * AXES + f, part_out[f].at[pl.ds(0, (LINE - 1) * ROWS), cols])


def hand_on(moe_in, attn_in, moe, attn, moe_held, attn_held, in_sem, out_sem):
    PIECES = 4
    steps = [(moe_in, moe_held, moe)]
    for i in range(PIECES):
        rows = pl.ds(i * (SESS // PIECES), SESS // PIECES)
        steps.append((attn_in.at[rows], attn_held.at[rows], attn.at[rows]))
    for i, (src, held, dst) in enumerate(steps):
        pltpu.make_async_copy(src, held, in_sem.at[i]).start()
    for i, (src, held, dst) in enumerate(steps):
        pltpu.make_async_copy(src, held, in_sem.at[i]).wait()
        pltpu.make_async_copy(held, dst, out_sem.at[i]).start()
    for i, (src, held, dst) in enumerate(steps):
        pltpu.make_async_copy(held, dst, out_sem.at[i]).wait()


def on_device(
    tokens, expert_ids, gate_weights, expert_gate, expert_up, expert_down, pool_latent, pool_rope,
    page_owner, page_index, lengths, query_latent, query_rope, new_latent, new_rope,
):
    vmem = pl.BlockSpec(memory_space=pltpu.VMEM)
    smem = pl.BlockSpec(memory_space=pltpu.SMEM)
    hbm = pl.BlockSpec(memory_space=pl.ANY)
    bf = jnp.bfloat16
    line_rows = [pltpu.VMEM((LINE * ROWS, w), bf) for w in WIDTH]
    slot_rows = [pltpu.VMEM((SLOTS, w), bf) for w in WIDTH]
    results = (
        jax.ShapeDtypeStruct((ROWS, D), bf),
        jax.ShapeDtypeStruct((SESS, HEADS, KV), bf),
    )
    held = pl.pallas_call(
        step_kernel,
        out_shape=results,
        in_specs=[vmem] * 4 + [smem] * 3 + [vmem] * 3 + [hbm] * 5,
        out_specs=(vmem, hbm),
        scratch_shapes=[
            pltpu.VMEM((SESS, PAGE, KV), bf),
            pltpu.VMEM((SESS, HEADS, KV), bf),
            pltpu.VMEM((SESS, HEADS, KV), bf),
            pltpu.VMEM((DEVS, 1, DEVS), jnp.int32),
            pltpu.SMEM((DEVS, 1, DEVS), jnp.int32),
            pltpu.VMEM((AXES, 2 * TOP, DEVS), jnp.float32),
            pltpu.VMEM((AXES * LINE, 2 * TOP, DEVS), jnp.float32),
            *line_rows, *slot_rows, *slot_rows, *slot_rows, *line_rows, *line_rows,
            pltpu.VMEM((AXES, 2 * DEVS, SLOTS), bf),
            pltpu.VMEM((AXES, DEVS, DEVS), jnp.float32),
            pltpu.VMEM((AXES, DEVS, DEVS), jnp.float32),
            pltpu.VMEM((SLOTS, D), bf),
            pltpu.VMEM((FF // FC, SLOTS, FC), bf),
            pltpu.VMEM((DEVS, PAGE, KV), bf),
            pltpu.VMEM((DEVS, PAGE, KV), bf),
            pltpu.VMEM((SESS, HALF, 2 * ROPE), bf),
            pltpu.VMEM((DEVS, HALF, 2 * ROPE), bf),
            pltpu.VMEM((DEVS, HALF, 2 * ROPE), bf),
            pltpu.VMEM((2, D, FC), bf),
            pltpu.VMEM((2, D, FC), bf),
            pltpu.VMEM((2, FF, WIDTH[0]), bf),
            pltpu.VMEM((PAIR, PMAX * PAGE, KV), bf),
            pltpu.VMEM((PAIR, PMAX * HALF, 2 * ROPE), bf),
            pltpu.VMEM((SESS, 2 * HEADS, 2 * ROPE), bf),
            pltpu.VMEM((SESS, HEADS, 2 * ROPE), jnp.float32),
            pltpu.VMEM((SESS, KV), jnp.float32),
            pltpu.VMEM((SESS, ROPE), jnp.float32),
            pltpu.VMEM((HEADS // 2 * SESS, 2 * ROPE), jnp.float32),
            pltpu.VMEM((HEADS // 2 * SESS, 2 * ROPE), jnp.float32),
            pltpu.SemaphoreType.DMA((PART + 2 * AXES,)),
            pltpu.SemaphoreType.DMA((PART + 2 * AXES,)),
            pltpu.SemaphoreType.DMA((PART + 2 * AXES,)),
            pltpu.SemaphoreType.DMA((2, 2)),
            pltpu.SemaphoreType.DMA((2,)),
            pltpu.SemaphoreType.DMA,
            pltpu.SemaphoreType.DMA,
            pltpu.SemaphoreType.DMA,
            pltpu.SemaphoreType.DMA,
        ],
        compiler_params=pltpu.CompilerParams(
            collective_id=0, has_side_effects=True, vmem_limit_bytes=62 * 2**20
        ),
    )(
        tokens, expert_ids.T, gate_weights.T, pool_rope, page_owner, page_index, lengths,
        query_rope, new_latent, new_rope, pool_latent, query_latent, expert_gate, expert_up,
        expert_down,
    )
    return pl.pallas_call(
        hand_on,
        out_shape=results,
        in_specs=[hbm] * 2,
        out_specs=(hbm, hbm),
        scratch_shapes=[
            pltpu.VMEM((ROWS, D), bf),
            pltpu.VMEM((SESS, HEADS, KV), bf),
            pltpu.SemaphoreType.DMA((5,)),
            pltpu.SemaphoreType.DMA((5,)),
        ],
    )(*held)


def solution(mesh):
    both = ("grp", "dev")
    in_specs = (
        P(both, None), P(both, None), P(both, None), P(both, None, None), P(both, None, None),
        P(both, None, None), P(both, None, None), P(both, None), P(both, None), P(both, None),
        P(both), P(both, None, None), P(both, None), P(both, None), P(both, None),
    )
    out_specs = (P(both, None), P(both, None, None))
    return jax.shard_map(
        on_device, mesh=mesh, in_specs=in_specs, out_specs=out_specs, check_vma=False
    )
```

```python
import jax
import jax.numpy as jnp
from jax import lax
from jax.experimental import pallas as pl
from jax.experimental.pallas import tpu as pltpu
from jax.sharding import PartitionSpec as P

MESH = pl.DeviceIdType.MESH
score_scale = 192.0 ** (-0.5)
neg_large = -1e30

DEVS = 128
MEMBERS = 32
ROWS = 32
TOP = 8
CAP = 4
D = 3584
FF = 1024
SESS = 16
HEADS = 64
KV = 512
ROPE = 64
PAGE = 64
PMAX = 16
HALF = PAGE // 2
FC = 256
WIDTH = (1280, 1152, 1152)
START = (0, 1280, 2432)
PAIR = 2
LATE = 256
AXES = 3
LINE = 4
PLANE = DEVS // LINE
SLOT = LINE * CAP
SLOTS = PLANE * SLOT
BLK = 256
EARLY = 12
NEAR = 8
REQ, LAT, ROP, META, AG, DISP, RET, PART = 0, 2, 3, 4, 5, 8, 11, 17
NT = (((1,), (1,)), ((), ()))


def f32_dot(a, b):
    return jnp.dot(a, b, preferred_element_type=jnp.float32)


def f32_dot_nt(a, b):
    return lax.dot_general(a, b, NT, preferred_element_type=jnp.float32)


def iota(shape, dim):
    return lax.broadcasted_iota(jnp.int32, shape, dim)


def ones_where(mask):
    return jnp.where(mask, 1.0, 0.0).astype(jnp.bfloat16)


def partner(g, d, k):
    core, z, x = lax.rem(d, 2), lax.rem(d // 2, 4), d // 8
    a, b, c, dc = lax.rem(k, 4), lax.rem(k // 4, 4), lax.rem(k // 16, 4), k // 64
    dx = lax.rem(a + 2 * core, 4)
    dy = lax.rem(dx + lax.rem(b + core, 4) + 1, 4)
    dz = lax.rem(dx + lax.rem(c + 3 * core, 4) + 2, 4)
    tg = lax.rem(g + dy, 4)
    td = lax.rem(x + dx, 4) * 8 + lax.rem(z + dz, 4) * 2 + lax.rem(core + dc, 2)
    return tg * MEMBERS + td


def plane_partner(a, b, core, k):
    da = lax.rem(k, 4) + 2 * core
    ta = lax.rem(a + da, 4)
    tb = lax.rem(b + da + lax.rem(k // 4, 4) + 1 + core, 4)
    return ta * 8 + tb * 2 + lax.rem(core + k // 16, 2)


def device_of(f, u, m):
    if f == 0:
        return u // 8 * 32 + m * 8 + lax.rem(u, 8)
    if f == 1:
        return m * 32 + u
    return u // 8 * 32 + lax.rem(u, 8) // 2 * 8 + m * 2 + lax.rem(u, 2)


def unfold(tiles, index):
    pairs = tiles[pl.ds(index, HEADS // 2, stride=SESS), :].astype(jnp.bfloat16)
    twice = f32_dot(
        ones_where(iota((HEADS, HEADS // 2), 0) // 2 == iota((HEADS, HEADS // 2), 1)), pairs
    )
    mine = iota((HEADS, 2 * ROPE), 1) // ROPE == lax.rem(iota((HEADS, 2 * ROPE), 0), 2)
    half = jnp.where(mine, twice, 0.0)
    return half + pltpu.roll(half, ROPE, 1)


def step_kernel(
    tokens, ids, gates, pool_rope, owner_sm, index_sm, len_sm, qr, nl, nr,
    pool_hbm, query_hbm, wg, wu, wd,
    moe, attn_hbm,
    pool_lat, ql, attn,
    req_in, req_sm, meta_out, meta_in,
    ag0, ag1, ag2, out0, out1, out2, in0, in1, in2, ret0, ret1, ret2,
    po0, po1, po2, pi0, pi1, pi2, gg, placed, weighed, xrows, hidden,
    lat_send, lat_recv, rope_pack, rope_send, rope_recv, wgb, wub, wdb, ks, rs, qrope, owns, nlf, nrf,
    qtiles, ptiles,
    send_sem, recv_sem, self_sem, up_sem, down_sem, sm_sem, pool_sem, query_sem, attn_sem,
):
    ag, disp_out, disp_in, ret_in = (ag0, ag1, ag2), (out0, out1, out2), (in0, in1, in2), (
        ret0, ret1, ret2,
    )
    part_out, part_in = (po0, po1, po2), (pi0, pi1, pi2)
    g = lax.axis_index("grp")
    d = lax.axis_index("dev")
    me = g * MEMBERS + d
    core, z, x = lax.rem(d, 2), lax.rem(d // 2, 4), d // 8
    across = ((g, z), (x, z), (g, x))
    along = (x, g, z)
    place = tuple(a * 8 + b * 2 + core for a, b in across)

    barrier = pltpu.get_barrier_semaphore()

    def greet(k, c):
        t = lax.rem(me + k, DEVS)
        pl.semaphore_signal(
            barrier, inc=1, device_id=(t // MEMBERS, lax.rem(t, MEMBERS)), device_id_type=MESH
        )
        return c

    lax.fori_loop(1, DEVS, greet, 0)

    pool_copy = pltpu.make_async_copy(pool_hbm, pool_lat, pool_sem)
    pool_copy.start()
    query_copy = pltpu.make_async_copy(query_hbm, ql, query_sem)
    query_copy.start()

    def up_copies(c, slot):
        cols = pl.ds(pl.multiple_of(c * FC, FC), FC)
        return (
            pltpu.make_async_copy(wg.at[0, :, cols], wgb.at[slot], up_sem.at[slot, 0]),
            pltpu.make_async_copy(wu.at[0, :, cols], wub.at[slot], up_sem.at[slot, 1]),
        )

    def down_copy(f):
        slot = f % 2
        return pltpu.make_async_copy(
            wd.at[0, :, pl.ds(START[f], WIDTH[f])],
            wdb.at[slot, :, pl.ds(0, WIDTH[f])],
            down_sem.at[slot],
        )

    for slot in range(2):
        for copy in up_copies(slot, slot):
            copy.start()
        down_copy(slot).start()

    lane = iota((1, DEVS), 1)

    def ask(s, asked):
        for p in range(PMAX):
            owner = jnp.where(p * PAGE < len_sm[s], owner_sm[s, p], -1)
            asked = jnp.where(lane == owner, index_sm[s, p], asked)
        return asked

    req_in[me] = lax.fori_loop(0, SESS, ask, jnp.zeros((1, DEVS), jnp.int32))

    choice = jnp.concatenate([ids[...].astype(jnp.float32), gates[...]], axis=0)
    choice = jnp.concatenate([choice] * LINE, axis=1)
    own_lanes = iota((2 * TOP, DEVS), 1) // ROWS
    for f in range(AXES):
        mine = jnp.where(own_lanes == along[f], choice, 0.0)
        meta_out[f] = mine
        meta_in[f * LINE + along[f]] = mine
        ag[f][pl.ds(pl.multiple_of(along[f] * ROWS, ROWS), ROWS), :] = tokens[
            :, START[f] : START[f] + WIDTH[f]
        ]

    for j in range(HEADS // 2):
        cols = slice(j * 2 * ROPE, (j + 1) * 2 * ROPE)
        ptiles[j * SESS : (j + 1) * SESS, :] = pool_rope[:, cols].astype(jnp.float32)
        qtiles[j * SESS : (j + 1) * SESS, :] = qr[:, cols].astype(jnp.float32)

    def pack(page, c):
        both = unfold(ptiles, page)
        first = iota((HALF, 2 * ROPE), 1) < ROPE
        rope_pack[page] = jnp.where(first, both[:HALF], both[HALF:]).astype(jnp.bfloat16)
        return c

    lax.fori_loop(0, SESS, pack, 0)
    nlf[...] = nl[...].astype(jnp.float32)
    nrf[...] = nr[...].astype(jnp.float32)

    pl.semaphore_wait(barrier, DEVS - 1)

    def send(index, src, dst, t):
        pltpu.make_async_remote_copy(
            src_ref=src, dst_ref=dst, send_sem=send_sem.at[index], recv_sem=recv_sem.at[index],
            device_id=(t // MEMBERS, lax.rem(t, MEMBERS)), device_id_type=MESH,
        ).start()

    def exchange(index, src, dst, t):
        @pl.when(t != me)
        def _():
            send(index, src, dst, t)

        @pl.when(t == me)
        def _():
            pltpu.make_async_copy(src, dst, self_sem.at[index]).start()

    def arrived(index, others, own=None):
        pltpu.make_async_copy(others, others, recv_sem.at[index]).wait()
        if own is not None:
            pltpu.make_async_copy(own, own, self_sem.at[index]).wait()

    def left(index, others):
        pltpu.make_async_copy(others, others, send_sem.at[index]).wait()

    def rows_of(t, size):
        return pl.ds(pl.multiple_of(t * size, size), size)

    near, far = lax.rem(me, NEAR), me // NEAR
    for h in range(1, NEAR):
        row = req_in.at[me]
        send(REQ, row, row, far * NEAR + lax.rem(near + h, NEAR))
    arrived(REQ, req_in.at[pl.ds(0, NEAR - 1)])

    def send_req(h, c):
        rows = req_in.at[rows_of(far, NEAR)]
        send(REQ + 1, rows, rows, lax.rem(far + h, DEVS // NEAR) * NEAR + near)
        return c

    lax.fori_loop(1, DEVS // NEAR, send_req, 0)
    for h in range(1, LINE):
        for f in range(AXES):
            t = device_of(f, place[f], lax.rem(along[f] + h, LINE))
            send(META, meta_out.at[f], meta_in.at[f * LINE + along[f]], t)
    for h in range(1, LINE):
        for f in range(AXES):
            t = device_of(f, place[f], lax.rem(along[f] + h, LINE))
            block = ag[f].at[rows_of(along[f], ROWS)]
            send(AG + f, block, block, t)

    arrived(REQ + 1, req_in.at[pl.ds(0, DEVS - NEAR)])
    to_sm = pltpu.make_async_copy(req_in, req_sm, sm_sem)
    to_sm.start()
    to_sm.wait()

    def send_page(k, c):
        t = partner(g, d, k)
        index = req_sm[t, 0, me]
        lat_send[t] = pool_lat[index]
        rope_send[t] = rope_pack[index]
        exchange(LAT, lat_send.at[t], lat_recv.at[me], t)
        exchange(ROP, rope_send.at[t], rope_recv.at[me], t)
        return c

    pool_copy.wait()
    lax.fori_loop(0, EARLY, send_page, 0)

    arrived(META, meta_in.at[pl.ds(0, AXES * (LINE - 1))])
    expert = iota((DEVS, DEVS), 0)
    from_row, to_row = expert, iota((DEVS, DEVS), 1)
    earlier = ones_where((from_row // ROWS == to_row // ROWS) & (from_row < to_row))
    for f in range(AXES):
        line = meta_in[f * LINE]
        for m in range(1, LINE):
            line = line + meta_in[f * LINE + m]
        chosen = line[:TOP].astype(jnp.int32)
        named = jnp.zeros((DEVS, DEVS), jnp.float32)
        weight = jnp.zeros((DEVS, DEVS), jnp.float32)
        for k in range(TOP):
            hit = chosen[k : k + 1] == expert
            named = named + jnp.where(hit, 1.0, 0.0)
            weight = weight + jnp.where(hit, line[TOP + k : TOP + k + 1], 0.0)
        rank = f32_dot(named.astype(jnp.bfloat16), earlier)
        placed[f] = named * (rank + 1.0)
        weighed[f] = weight

    for f in range(AXES):
        arrived(AG + f, ag[f].at[pl.ds(0, (LINE - 1) * ROWS)])
        for b in range(SLOTS // BLK):
            row = iota((BLK, DEVS), 0) + b * BLK
            col = iota((BLK, DEVS), 1)
            spread = ones_where(col == device_of(f, row // SLOT, along[f]))
            at = f32_dot(spread, placed[f].astype(jnp.bfloat16))
            want = (lax.rem(row, CAP) + 1).astype(jnp.float32)
            pick = ones_where((at == want) & (lax.rem(row // CAP, LINE) == col // ROWS))
            disp_out[f][b * BLK : (b + 1) * BLK, :] = f32_dot(pick, ag[f][...]).astype(
                jnp.bfloat16
            )

    def send_disp(k, c):
        for f in range(AXES):
            u = plane_partner(*across[f], core, k)
            exchange(
                DISP + f, disp_out[f].at[rows_of(u, SLOT)], disp_in[f].at[rows_of(place[f], SLOT)],
                device_of(f, u, along[f]),
            )
        return c

    lax.fori_loop(0, PLANE, send_disp, 0)
    lax.fori_loop(EARLY, DEVS, send_page, 0)

    for f in range(AXES):
        row = iota((DEVS, SLOTS), 0)
        col = iota((DEVS, SLOTS), 1)
        spread = ones_where(row == device_of(f, col // SLOT, along[f]))
        at = f32_dot(placed[f].T.astype(jnp.bfloat16), spread)
        want = (lax.rem(col, CAP) + 1).astype(jnp.float32)
        keep = (at == want) & (lax.rem(col // CAP, LINE) == row // ROWS)
        weight = weighed[f].T
        high = weight.astype(jnp.bfloat16)
        low = (weight - high.astype(jnp.float32)).astype(jnp.bfloat16)
        gg[f, 0:DEVS, :] = jnp.where(keep, f32_dot(high, spread), 0.0).astype(jnp.bfloat16)
        gg[f, DEVS:, :] = jnp.where(keep, f32_dot(low, spread), 0.0).astype(jnp.bfloat16)

    query_copy.wait()

    def prepare(s, c):
        qd = unfold(qtiles, s)
        first = iota((HEADS, 2 * ROPE), 1) < ROPE
        qrope[s, :HEADS] = jnp.where(first, qd, 0.0).astype(jnp.bfloat16)
        qrope[s, HEADS:] = jnp.where(first, 0.0, qd).astype(jnp.bfloat16)
        own = jnp.sum(ql[s].astype(jnp.float32) * nlf[pl.ds(s, 1), :], axis=1, keepdims=True)
        own = own + jnp.sum(qd[:, :ROPE] * nrf[pl.ds(s, 1), :], axis=1, keepdims=True)
        owns[s] = jnp.broadcast_to(own * score_scale, (HEADS, 2 * ROPE))
        return c

    lax.fori_loop(0, SESS, prepare, 0)

    def source_row(f, at):
        return device_of(f, at // SLOT, lax.rem(at // CAP, LINE)) * CAP + lax.rem(at, CAP)

    for f in range(AXES):
        arrived(
            DISP + f, disp_in[f].at[pl.ds(0, SLOTS - SLOT)], disp_in[f].at[pl.ds(0, SLOT)]
        )
        goes_to = source_row(f, iota((1, SLOTS), 1))
        for b in range(SLOTS // BLK):
            order = ones_where(iota((BLK, SLOTS), 0) + b * BLK == goes_to)
            xrows[b * BLK : (b + 1) * BLK, START[f] : START[f] + WIDTH[f]] = f32_dot(
                order, disp_in[f][...]
            ).astype(jnp.bfloat16)

    def up(c, carry):
        slot = lax.rem(c, 2)
        for copy in up_copies(c, slot):
            copy.wait()
        gate_proj = f32_dot(xrows[...], wgb[slot])
        up_proj = f32_dot(xrows[...], wub[slot])
        hidden[c] = (gate_proj / (1.0 + jnp.exp(-gate_proj)) * up_proj).astype(jnp.bfloat16)

        @pl.when(c + 2 < FF // FC)
        def _():
            for copy in up_copies(c + 2, slot):
                copy.start()

        return carry

    lax.fori_loop(0, FF // FC, up, 0)

    for f in range(AXES):
        down_copy(f).wait()
        slot = f % 2
        total = f32_dot(hidden[0], wdb[slot, 0:FC, 0 : WIDTH[f]])
        for c in range(1, FF // FC):
            total = total + f32_dot(hidden[c], wdb[slot, c * FC : (c + 1) * FC, 0 : WIDTH[f]])
        xrows[:, START[f] : START[f] + WIDTH[f]] = total.astype(jnp.bfloat16)
        if f + 2 < AXES:
            down_copy(f + 2).start()
        for b in range(SLOTS // BLK):
            comes_from = source_row(f, iota((BLK, 1), 0) + b * BLK)
            order = ones_where(iota((BLK, SLOTS), 1) == comes_from)
            disp_in[f][b * BLK : (b + 1) * BLK, :] = f32_dot(
                order, xrows[:, START[f] : START[f] + WIDTH[f]]
            ).astype(jnp.bfloat16)

    def columns(f, turn):
        return pl.ds(0, WIDTH[f] - LATE) if turn == 0 else pl.ds(WIDTH[f] - LATE, LATE)

    for turn in range(2):

        def send_ret(k, c, turn=turn):
            for f in range(AXES):
                u = plane_partner(*across[f], core, k)
                cols = columns(f, turn)
                exchange(
                    RET + turn * AXES + f, disp_in[f].at[rows_of(u, SLOT), cols],
                    ret_in[f].at[rows_of(place[f], SLOT), cols], device_of(f, u, along[f]),
                )
            return c

        lax.fori_loop(0, PLANE, send_ret, 0)

    arrived(LAT, lat_recv.at[pl.ds(0, DEVS - 1)], lat_recv.at[0])
    arrived(ROP, rope_recv.at[pl.ds(0, DEVS - 1)], rope_recv.at[0])
    LM = PMAX * PAGE

    def session(s, held):
        for p in range(PMAX):
            owner = owner_sm[s, p]
            page = lat_recv[owner]
            ks[held, p * HALF : (p + 1) * HALF, :] = page[:HALF]
            ks[held, LM // 2 + p * HALF : LM // 2 + (p + 1) * HALF, :] = page[HALF:]
            rs[held, p * HALF : (p + 1) * HALF, :] = rope_recv[owner]
        both = f32_dot_nt(qrope[s], rs[held])
        rope_scores = jnp.concatenate([both[:HEADS], both[HEADS:]], axis=1)
        scores = (f32_dot_nt(ql[s], ks[held]) + rope_scores) * score_scale
        own = owns[s][:, :1]
        at = iota((1, LM), 1)
        rest = lax.rem(at, LM // 2)
        position = rest // HALF * PAGE + at // (LM // 2) * HALF + lax.rem(rest, HALF)
        visible = position < len_sm[s]
        masked = jnp.where(visible, scores, neg_large)
        top = jnp.maximum(jnp.max(masked, axis=1, keepdims=True), own)
        weights = jnp.where(visible, jnp.exp(masked - top), 0.0)
        own_weight = jnp.exp(own - top)
        denominator = jnp.sum(weights, axis=1, keepdims=True) + own_weight
        blended = f32_dot(weights.astype(jnp.bfloat16), ks[held])
        own_weight = own_weight.astype(jnp.bfloat16).astype(jnp.float32)
        blended = blended + own_weight * nlf[pl.ds(s, 1), :]
        attn[s] = (blended / denominator).astype(jnp.bfloat16)

    def sessions(i, c):
        for held in range(PAIR):
            session(i * PAIR + held, held)
        return c

    lax.fori_loop(0, SESS // PAIR, sessions, 0)
    attn_copy = pltpu.make_async_copy(attn, attn_hbm, attn_sem)
    attn_copy.start()

    def add_line(f, turn):
        index = RET + turn * AXES + f
        cols = columns(f, turn)
        arrived(
            index, ret_in[f].at[pl.ds(0, SLOTS - SLOT), cols], ret_in[f].at[pl.ds(0, SLOT), cols]
        )
        both = f32_dot(gg[f], ret_in[f][:, cols])
        part_out[f][:, cols] = (both[:DEVS] + both[DEVS:]).astype(jnp.bfloat16)
        index = PART + turn * AXES + f
        for h in range(LINE):
            m = lax.rem(along[f] + h, LINE)
            src = part_out[f].at[rows_of(m, ROWS), cols]
            dst = part_in[f].at[rows_of(along[f], ROWS), cols]
            if h == 0:
                pltpu.make_async_copy(src, dst, self_sem.at[index]).start()
            else:
                send(index, src, dst, device_of(f, place[f], m))

    def add_parts(f, turn):
        cols = columns(f, turn)
        arrived(
            PART + turn * AXES + f, part_in[f].at[pl.ds(0, (LINE - 1) * ROWS), cols],
            part_in[f].at[pl.ds(0, ROWS), cols],
        )
        total = part_in[f][0:ROWS, cols].astype(jnp.float32)
        for m in range(1, LINE):
            total = total + part_in[f][m * ROWS : (m + 1) * ROWS, cols].astype(jnp.float32)
        moe[:, pl.ds(START[f] + cols.start, cols.size)] = total.astype(jnp.bfloat16)

    for f in range(AXES):
        add_line(f, 0)

    left(REQ, req_in.at[pl.ds(0, NEAR - 1)])
    left(REQ + 1, req_in.at[pl.ds(0, DEVS - NEAR)])
    left(LAT, lat_send.at[pl.ds(0, DEVS - 1)])
    left(ROP, rope_send.at[pl.ds(0, DEVS - 1)])
    left(META, meta_in.at[pl.ds(0, AXES * (LINE - 1))])
    for f in range(AXES):
        left(AG + f, ag[f].at[pl.ds(0, (LINE - 1) * ROWS)])
        left(DISP + f, disp_out[f].at[pl.ds(0, SLOTS - SLOT)])
        left(RET + f, disp_in[f].at[pl.ds(0, SLOTS - SLOT), columns(f, 0)])

    for f in range(AXES):
        add_line(f, 1)
    for f in range(AXES):
        add_parts(f, 0)
        left(RET + AXES + f, disp_in[f].at[pl.ds(0, SLOTS - SLOT), columns(f, 1)])
    for f in range(AXES):
        add_parts(f, 1)

    attn_copy.wait()
    for f in range(AXES):
        for turn in range(2):
            cols = columns(f, turn)
            left(PART + turn * AXES + f, part_out[f].at[pl.ds(0, (LINE - 1) * ROWS), cols])


def hand_on(moe_in, attn_in, moe, attn, moe_held, attn_held, in_sem, out_sem):
    PIECES = 4
    steps = [(moe_in, moe_held, moe)]
    for i in range(PIECES):
        rows = pl.ds(i * (SESS // PIECES), SESS // PIECES)
        steps.append((attn_in.at[rows], attn_held.at[rows], attn.at[rows]))
    for i, (src, held, dst) in enumerate(steps):
        pltpu.make_async_copy(src, held, in_sem.at[i]).start()
    for i, (src, held, dst) in enumerate(steps):
        pltpu.make_async_copy(src, held, in_sem.at[i]).wait()
        pltpu.make_async_copy(held, dst, out_sem.at[i]).start()
    for i, (src, held, dst) in enumerate(steps):
        pltpu.make_async_copy(held, dst, out_sem.at[i]).wait()


def on_device(
    tokens, expert_ids, gate_weights, expert_gate, expert_up, expert_down, pool_latent, pool_rope,
    page_owner, page_index, lengths, query_latent, query_rope, new_latent, new_rope,
):
    vmem = pl.BlockSpec(memory_space=pltpu.VMEM)
    smem = pl.BlockSpec(memory_space=pltpu.SMEM)
    hbm = pl.BlockSpec(memory_space=pl.ANY)
    bf = jnp.bfloat16
    line_rows = [pltpu.VMEM((LINE * ROWS, w), bf) for w in WIDTH]
    slot_rows = [pltpu.VMEM((SLOTS, w), bf) for w in WIDTH]
    results = (
        jax.ShapeDtypeStruct((ROWS, D), bf),
        jax.ShapeDtypeStruct((SESS, HEADS, KV), bf),
    )
    held = pl.pallas_call(
        step_kernel,
        out_shape=results,
        in_specs=[vmem] * 4 + [smem] * 3 + [vmem] * 3 + [hbm] * 5,
        out_specs=(vmem, hbm),
        scratch_shapes=[
            pltpu.VMEM((SESS, PAGE, KV), bf),
            pltpu.VMEM((SESS, HEADS, KV), bf),
            pltpu.VMEM((SESS, HEADS, KV), bf),
            pltpu.VMEM((DEVS, 1, DEVS), jnp.int32),
            pltpu.SMEM((DEVS, 1, DEVS), jnp.int32),
            pltpu.VMEM((AXES, 2 * TOP, DEVS), jnp.float32),
            pltpu.VMEM((AXES * LINE, 2 * TOP, DEVS), jnp.float32),
            *line_rows, *slot_rows, *slot_rows, *slot_rows, *line_rows, *line_rows,
            pltpu.VMEM((AXES, 2 * DEVS, SLOTS), bf),
            pltpu.VMEM((AXES, DEVS, DEVS), jnp.float32),
            pltpu.VMEM((AXES, DEVS, DEVS), jnp.float32),
            pltpu.VMEM((SLOTS, D), bf),
            pltpu.VMEM((FF // FC, SLOTS, FC), bf),
            pltpu.VMEM((DEVS, PAGE, KV), bf),
            pltpu.VMEM((DEVS, PAGE, KV), bf),
            pltpu.VMEM((SESS, HALF, 2 * ROPE), bf),
            pltpu.VMEM((DEVS, HALF, 2 * ROPE), bf),
            pltpu.VMEM((DEVS, HALF, 2 * ROPE), bf),
            pltpu.VMEM((2, D, FC), bf),
            pltpu.VMEM((2, D, FC), bf),
            pltpu.VMEM((2, FF, WIDTH[0]), bf),
            pltpu.VMEM((PAIR, PMAX * PAGE, KV), bf),
            pltpu.VMEM((PAIR, PMAX * HALF, 2 * ROPE), bf),
            pltpu.VMEM((SESS, 2 * HEADS, 2 * ROPE), bf),
            pltpu.VMEM((SESS, HEADS, 2 * ROPE), jnp.float32),
            pltpu.VMEM((SESS, KV), jnp.float32),
            pltpu.VMEM((SESS, ROPE), jnp.float32),
            pltpu.VMEM((HEADS // 2 * SESS, 2 * ROPE), jnp.float32),
            pltpu.VMEM((HEADS // 2 * SESS, 2 * ROPE), jnp.float32),
            pltpu.SemaphoreType.DMA((PART + 2 * AXES,)),
            pltpu.SemaphoreType.DMA((PART + 2 * AXES,)),
            pltpu.SemaphoreType.DMA((PART + 2 * AXES,)),
            pltpu.SemaphoreType.DMA((2, 2)),
            pltpu.SemaphoreType.DMA((2,)),
            pltpu.SemaphoreType.DMA,
            pltpu.SemaphoreType.DMA,
            pltpu.SemaphoreType.DMA,
            pltpu.SemaphoreType.DMA,
        ],
        compiler_params=pltpu.CompilerParams(
            collective_id=0, has_side_effects=True, vmem_limit_bytes=62 * 2**20
        ),
    )(
        tokens, expert_ids.T, gate_weights.T, pool_rope, page_owner, page_index, lengths,
        query_rope, new_latent, new_rope, pool_latent, query_latent, expert_gate, expert_up,
        expert_down,
    )
    return pl.pallas_call(
        hand_on,
        out_shape=results,
        in_specs=[hbm] * 2,
        out_specs=(hbm, hbm),
        scratch_shapes=[
            pltpu.VMEM((ROWS, D), bf),
            pltpu.VMEM((SESS, HEADS, KV), bf),
            pltpu.SemaphoreType.DMA((5,)),
            pltpu.SemaphoreType.DMA((5,)),
        ],
    )(*held)


def solution(mesh):
    both = ("grp", "dev")
    in_specs = (
        P(both, None), P(both, None), P(both, None), P(both, None, None), P(both, None, None),
        P(both, None, None), P(both, None, None), P(both, None), P(both, None), P(both, None),
        P(both), P(both, None, None), P(both, None), P(both, None), P(both, None),
    )
    out_specs = (P(both, None), P(both, None, None))
    return jax.shard_map(
        on_device, mesh=mesh, in_specs=in_specs, out_specs=out_specs, check_vma=False
    )
```
